32 devices in a mesh: dp: 4 (over x, core), sp: 8 (over z, y).
Axes of the slice: x: 2, y: 2, z: 4, core: 2. Of those that a mesh axis runs over, the one named last changes fastest.
Arguments:
- frames_in: bfloat16 [2048, 64, 256], P(('dp', 'sp')), may hold values from -6 to 6
- spatial_weight: bfloat16 [3, 3, 256, 256], replicated, may hold values from -0.125 to 0.125
- temporal_weight: bfloat16 [3, 256, 256], replicated, may hold values from -0.21875 to 0.21875
- cotangent: bfloat16 [2048, 64, 256], P(('dp', 'sp')), may hold values from -6 to 6
Outputs:
- block_out: bfloat16 [2048, 64, 256], P(('dp', 'sp'))
- grad_input: bfloat16 [2048, 64, 256], P(('dp', 'sp'))
- grad_spatial: float32 [3, 3, 256, 256], replicated
- grad_temporal: float32 [3, 256, 256], replicated
The draws below stay inside these ranges and needn't reach their ends.
All inputs are finite; a program needn't handle non-finite values.
Results may differ from the reference program's by a relative error of at most 0.0049.
Values may be sent and summed in bfloat16 or wider, within the bound.
A program may use at most 128 MiB of HBM per device.

```python
import math
import jax
import jax.numpy as jnp

C = 256
H = 64
W = 64
FRAMES = 4
ROWS = 2048


def levels(stream_key, dims, split, low, top_value):
    factor_of, own = 1.0, jax.random.fold_in(stream_key, 6)
    for dim, blocks in split:
        draws = jnp.exp(jax.random.uniform(jax.random.fold_in(own, dim), (blocks,), jnp.float32, low / len(split), top_value / len(split)))
        factor_of = factor_of * jnp.repeat(draws, dims[dim] // blocks).reshape([-1 if axis == dim else 1 for axis in range(len(dims))])
    return factor_of


def noise(rng, shape, scale, most, pieces=(), kind=jnp.bfloat16):
    values = jax.random.normal(rng, shape, jnp.float32) * scale
    if len(pieces) > 0:
        values = levels(rng, shape, pieces, -0.22, 0.18) * values
    return jnp.clip(values, min=-most, max=most).astype(kind)


def setup_inputs(seed: int = 0) -> dict:
    seeds = jax.random.split(jax.random.key(seed), 5)
    frames_in = noise(seeds[0], (ROWS, W, C), 1.0, 6.0, ((0, 32),))
    spatial_weight = noise(seeds[1], (3, 3, C, C), (9 * C) ** -0.5, 0.125)
    temporal_weight = noise(seeds[2], (3, C, C), (3 * C) ** -0.5, 0.21875)
    cotangent = noise(seeds[3], (ROWS, W, C), 1.0, 6.0, ((0, 32),))
    return {"frames_in": frames_in, "spatial_weight": spatial_weight, "temporal_weight": temporal_weight, "cotangent": cotangent}


def reference(frames_in, spatial_weight, temporal_weight, cotangent):
    total_rows, width_cells, channels = frames_in.shape
    frame_count = total_rows // H
    clip_count = frame_count // FRAMES
    frames_grid = frames_in.reshape(frame_count, H, width_cells, channels)
    padded_in = jnp.pad(frames_grid, ((0, 0), (1, 1), (1, 1), (0, 0)))
    pre = jnp.zeros((frame_count * H * width_cells, channels), jnp.float32)
    for tap_row in range(3):
        for tap_col in range(3):
            window = padded_in[:, tap_row:tap_row + H, tap_col:tap_col + width_cells].reshape(-1, channels)
            pre = pre + jnp.dot(window, spatial_weight[tap_row, tap_col], preferred_element_type=jnp.float32)
    act = jax.nn.silu(pre).astype(jnp.bfloat16)
    act_clips = act.reshape(clip_count, FRAMES, H * width_cells, channels)
    act_padded = jnp.pad(act_clips, ((0, 0), (2, 0), (0, 0), (0, 0)))
    cot_clips = cotangent.reshape(clip_count, FRAMES, H * width_cells, channels)
    cot_padded = jnp.pad(cot_clips, ((0, 0), (0, 2), (0, 0), (0, 0)))
    cot_flat = cotangent.reshape(-1, channels)
    temporal_out = jnp.zeros((total_rows * width_cells, channels), jnp.float32)
    grad_act = jnp.zeros((total_rows * width_cells, channels), jnp.float32)
    temporal_terms = []
    for tap_step in range(3):
        earlier = act_padded[:, 2 - tap_step:2 - tap_step + FRAMES].reshape(-1, channels)
        temporal_out = temporal_out + jnp.dot(earlier, temporal_weight[tap_step], preferred_element_type=jnp.float32)
        temporal_terms.append(jnp.dot(earlier.T, cot_flat, preferred_element_type=jnp.float32))
        later = cot_padded[:, tap_step:tap_step + FRAMES].reshape(-1, channels)
        grad_act = grad_act + jnp.dot(later, temporal_weight[tap_step].T, preferred_element_type=jnp.float32)
    temporal_out = temporal_out.astype(jnp.bfloat16)
    block_out = (frames_in.reshape(-1, channels).astype(jnp.float32) + temporal_out.astype(jnp.float32)).astype(jnp.bfloat16)
    grad_act = grad_act.astype(jnp.bfloat16)
    sigma = jax.nn.sigmoid(pre)
    grad_pre = (grad_act.astype(jnp.float32) * (sigma * (1.0 + pre * (1.0 - sigma)))).astype(jnp.bfloat16)
    grad_flat = grad_pre.reshape(-1, channels)
    grad_grid = grad_pre.reshape(frame_count, H, width_cells, channels)
    grad_padded = jnp.pad(grad_grid, ((0, 0), (1, 1), (1, 1), (0, 0)))
    spatial_terms = []
    grad_in = cot_flat.astype(jnp.float32)
    for tap_row in range(3):
        for tap_col in range(3):
            window = padded_in[:, tap_row:tap_row + H, tap_col:tap_col + width_cells].reshape(-1, channels)
            spatial_terms.append(jnp.dot(window.T, grad_flat, preferred_element_type=jnp.float32))
            back_window = grad_padded[:, 2 - tap_row:2 - tap_row + H, 2 - tap_col:2 - tap_col + width_cells].reshape(-1, channels)
            grad_in = grad_in + jnp.dot(back_window, spatial_weight[tap_row, tap_col].T, preferred_element_type=jnp.float32)
    grad_scale = 1.0 / math.sqrt(total_rows * width_cells)
    grad_spatial = jnp.stack(spatial_terms).reshape(3, 3, channels, channels) * grad_scale
    grad_temporal = jnp.stack(temporal_terms) * grad_scale
    shape_out = (total_rows, width_cells, channels)
    return (block_out.reshape(shape_out), grad_in.astype(jnp.bfloat16).reshape(shape_out), grad_spatial, grad_temporal)
```

```python
import functools
import math

import jax
import jax.numpy as jnp
from jax import lax
from jax.experimental import pallas as pl
from jax.experimental.pallas import tpu as pltpu
from jax.sharding import PartitionSpec as P

FRAMES = 4
CHUNKS = 8
HALF = CHUNKS // 2
VMEM_LIMIT = 58 * 1024 * 1024
MESH = pl.DeviceIdType.MESH
F32 = jnp.float32
BF16 = jnp.bfloat16


def mm(left, right):
    return jnp.dot(left, right, preferred_element_type=F32)


def store_shifted(dest, offset, values, width):
    cells, channels = values.shape
    column = lax.broadcasted_iota(jnp.int32, (cells, channels), 0) % width
    before = jnp.where(column == 0, 0.0, pltpu.roll(values, 1, axis=0))
    after = jnp.where(column == width - 1, 0.0, pltpu.roll(values, cells - 1, axis=0))
    dest[pl.ds(offset, cells), 0:channels] = before.astype(BF16)
    dest[pl.ds(offset, cells), channels : 2 * channels] = values.astype(BF16)
    dest[pl.ds(offset, cells), 2 * channels : 3 * channels] = after.astype(BF16)


def zero_edges(dest, width):
    rows, lanes = dest.shape
    dest[0:width] = jnp.zeros((width, lanes), BF16)
    dest[rows - width : rows] = jnp.zeros((width, lanes), BF16)


def block_kernel(
    width, members, scale,
    x_hbm, cot_hbm, w_ref, tw_ref,
    out_ref, gin_ref, full,
    x, cot, c1, c2, a1, a2, act, slope, x3, g3, wf, wt, part, acc,
    core_in, total, stage, x_in1, x_in2, z_in1, z_in2, slots,
    load_sem, c1_sem, c2_sem, a1_sem, a2_sem, cy_sem, cz_sem, ay_sem, az_sem, rc_sem, ra_sem,
    red_send, red_recv,
):
    dp = lax.axis_index("dp")
    sp = lax.axis_index("sp")
    frame = sp % FRAMES
    y = sp % 2
    zi = (sp // 2) % 4
    group = sp // 8
    member = y + 2 * group
    core = dp % 2
    mx = (dp // 2) % 2
    cells, channels = out_ref.shape
    size = cells // CHUNKS
    lanes = channels // 2

    y_dev = (dp, sp + 1 - 2 * y)
    t_dev = (dp, sp + 2 - 4 * (zi % 2))
    core_dev = (dp + 1 - 2 * core, sp)
    x_dev = (dp + 2 - 4 * mx, sp)

    def z_member(offset):
        return (zi + offset) % 4

    def z_dev(offset):
        return (dp, sp + (z_member(offset) - zi) * 2)

    def m_dev(offset):
        other = (member + offset) % members
        return (dp, sp + other % 2 - y + (other // 2 - group) * 8)

    def chunk(ref, index):
        return ref.at[pl.ds(pl.multiple_of(index * size, size), size), :]

    def copy(source, dest, send_sem, recv_sem, device):
        return pltpu.make_async_remote_copy(
            src_ref=source, dst_ref=dest, send_sem=send_sem, recv_sem=recv_sem,
            device_id=device, device_id_type=MESH,
        )

    def send(source, dest, index, send_sems, recv_sems, device):
        copy(
            chunk(source, index), chunk(dest, index), send_sems.at[index], recv_sems.at[index], device
        ).start()

    def arrived(dest, index, recv_sems):
        copy(
            chunk(dest, index), chunk(dest, index), recv_sems.at[index], recv_sems.at[index], y_dev
        ).wait_recv()

    def left(index, send_sems):
        copy(
            chunk(act, index), chunk(act, index), send_sems.at[index], send_sems.at[index], y_dev
        ).wait_send()

    def each(start, stop, body):
        def step(index, carry):
            body(index)
            return carry

        lax.fori_loop(start, stop, step, 0)

    x_load = pltpu.make_async_copy(x_hbm, x, load_sem.at[0])
    cot_load = pltpu.make_async_copy(cot_hbm, cot, load_sem.at[1])
    x_load.start()
    cot_load.start()

    barrier = pltpu.get_barrier_semaphore()
    greeted = [core_dev, x_dev] + [z_dev(i) for i in (1, 2, 3)] + [m_dev(i) for i in range(1, members)]
    for device in greeted:
        pl.semaphore_signal(barrier, inc=1, device_id=device, device_id_type=MESH)
    pl.semaphore_wait(barrier, len(greeted))

    @pl.when(frame == 1)
    def _():
        each(0, CHUNKS, lambda i: send(cot_hbm, c1, i, cy_sem, c1_sem, y_dev))

    @pl.when(frame == 2)
    def _():
        each(0, CHUNKS, lambda i: send(cot_hbm, c2, i, cz_sem, c2_sem, t_dev))
        each(HALF, CHUNKS, lambda i: send(cot_hbm, c1, i, cy_sem, c1_sem, y_dev))

    @pl.when(frame == 3)
    def _():
        each(0, CHUNKS, lambda i: send(cot_hbm, c1, i, cy_sem, c1_sem, y_dev))
        each(0, HALF, lambda i: send(cot_hbm, c2, i, cz_sem, c2_sem, t_dev))

    acc[...] = jnp.zeros_like(acc)
    zero_edges(x3, width)
    zero_edges(g3, width)
    x_load.wait()

    def forward(step):
        @pl.when(step < CHUNKS)
        def _():
            store_shifted(
                x3, pl.multiple_of(width + step * size, width),
                x[pl.ds(pl.multiple_of(step * size, size), size), :].astype(F32), width,
            )

        @pl.when(step >= 1)
        def _():
            index = step - 1
            base = pl.multiple_of(index * size, size)
            pre = jnp.zeros((size, channels), F32)
            for tap in range(3):
                pre = pre + mm(x3[pl.ds(base + tap * width, size), :], w_ref[tap])
            sigma = jax.nn.sigmoid(pre)
            act[pl.ds(base, size), :] = (pre * sigma).astype(BF16)
            slope[pl.ds(base, size), :] = sigma * (1.0 + pre * (1.0 - sigma))

            @pl.when(frame == 0)
            def _():
                send(act, a2, index, az_sem, a2_sem, t_dev)

            @pl.when((frame == 0) & (index == 0))
            def _():
                send(act, a1, index, ay_sem, a1_sem, y_dev)

            @pl.when((frame == 1) & (index < HALF))
            def _():
                send(act, a1, index, ay_sem, a1_sem, y_dev)

            @pl.when((frame == 1) & (index >= HALF))
            def _():
                send(act, a2, index, az_sem, a2_sem, t_dev)

            @pl.when(frame == 2)
            def _():
                send(act, a1, index, ay_sem, a1_sem, y_dev)

    each(0, CHUNKS + 1, forward)

    @pl.when(frame == 1)
    def _():
        each(0, HALF, lambda i: send(act, a2, i, az_sem, a2_sem, t_dev))

    for tap in range(3):
        wt[tap] = tw_ref[tap].T
        for side in range(3):
            wf[tap, side * channels : (side + 1) * channels, :] = w_ref[
                2 - tap, (2 - side) * channels : (3 - side) * channels, :
            ].T
    cot_load.wait()

    gt_base = 9 * channels

    def add_temporal(tap, act_t, other):
        acc[gt_base + tap * channels : gt_base + (tap + 1) * channels, :] += mm(act_t, other)

    def backward(index):
        base = pl.multiple_of(index * size, size)
        rows = pl.ds(base, size)
        early = index < HALF

        @pl.when((frame < 3) | (index >= HALF))
        def _():
            arrived(c1, index, c1_sem)

        @pl.when((frame == 0) | ((frame == 1) & early))
        def _():
            arrived(c2, index, c2_sem)

        @pl.when((frame == 0) & early)
        def _():
            send(c2, c1, index, rc_sem, c1_sem, y_dev)

        @pl.when((frame == 0) & (index == HALF - 1))
        def _():
            each(1, CHUNKS, lambda i: send(act, a1, i, ay_sem, a1_sem, y_dev))

        @pl.when((frame == 3) & (index >= HALF))
        def _():
            c2[rows, :] = (mm(c1[rows, :], wt[1]) + mm(cot[rows, :], wt[2])).astype(BF16)
            send(c2, c1, index, cz_sem, c1_sem, t_dev)

        act_t = act[rows, :].T
        part[...] = mm(cot[rows, :], wt[0])
        add_temporal(0, act_t, cot[rows, :])

        @pl.when((frame == 0) | (frame == 2) | ((frame == 1) & early))
        def _():
            part[...] += mm(c1[rows, :], wt[1])
            add_temporal(1, act_t, c1[rows, :])

        @pl.when((frame == 0) | ((frame == 1) & early))
        def _():
            part[...] += mm(c2[rows, :], wt[2])
            add_temporal(2, act_t, c2[rows, :])

        @pl.when((frame == 1) & (index >= HALF))
        def _():
            part[...] += c1[rows, :].astype(F32)

        grad_pre = part[...].astype(BF16).astype(F32) * slope[rows, :]
        store_shifted(g3, pl.multiple_of(width + base, width), grad_pre, width)
        grad_pre = grad_pre.astype(BF16)
        for tap in range(3):
            window = x3[pl.ds(base + tap * width, size), :]
            acc[tap * 3 * channels : (tap + 1) * 3 * channels, :] += mm(window.T, grad_pre)

    each(0, CHUNKS, backward)

    @pl.when(frame == 3)
    def _():
        def late(index):
            rows = pl.ds(pl.multiple_of(index * size, size), size)
            arrived(a2, index, a2_sem)
            send(a2, a1, index, ra_sem, a1_sem, y_dev)
            act_t = a2[rows, :].T
            add_temporal(1, act_t, c1[rows, :])
            add_temporal(2, act_t, cot[rows, :])

        each(HALF, CHUNKS, late)

    def relay(index):
        @pl.when(frame == 0)
        def _():
            arrived(a1, index, a1_sem)
            send(a1, a1, index, ra_sem, a1_sem, t_dev)

    def grad_input(index):
        base = pl.multiple_of(index * size, size)
        total_in = cot[pl.ds(base, size), :].astype(F32)
        for tap in range(3):
            total_in = total_in + mm(g3[pl.ds(base + tap * width, size), :], wf[tap])
        gin_ref[pl.ds(base, size), :] = total_in.astype(BF16)

    def output(index):
        rows = pl.ds(pl.multiple_of(index * size, size), size)

        @pl.when(frame >= 1)
        def _():
            arrived(a1, index, a1_sem)

        @pl.when((frame == 2) | ((frame == 3) & (index < HALF)))
        def _():
            arrived(a2, index, a2_sem)

        part[...] = mm(act[rows, :], tw_ref[0])

        @pl.when(frame >= 1)
        def _():
            part[...] += mm(a1[rows, :], tw_ref[1])

        @pl.when(frame >= 2)
        def _():
            part[...] += mm(a2[rows, :], tw_ref[2])

        temporal = part[...].astype(BF16).astype(F32)
        out_ref[rows, :] = (x[rows, :].astype(F32) + temporal).astype(BF16)

    count = acc.shape[0]
    n1 = count // 3 * 2
    h1, q1 = n1 // 2, n1 // 8
    q2 = (count - n1) // 4
    e2 = q2 // 2
    keep = pl.multiple_of(core * lanes, lanes)
    give = pl.multiple_of((1 - core) * lanes, lanes)
    used = []

    def exchange(source, dest, device):
        slot = len(used)
        moved = copy(source, dest, red_send.at[slot], red_recv.at[slot], device)
        moved.start()
        used.append(moved)
        return moved

    def rows_of(start, length):
        return pl.ds(pl.multiple_of(start, 16), length)

    own_half, other_half = rows_of(mx * h1, h1), rows_of((1 - mx) * h1, h1)

    def piece1(offset):
        return rows_of(mx * h1 + z_member(offset) * q1, q1)

    def piece2(offset):
        return rows_of(n1 + z_member(offset) * q2, q2)

    def quarter2(which):
        return rows_of(n1 + zi * q2 + which * e2, e2)

    moves = [exchange(acc.at[:, pl.ds(give, lanes)], core_in, core_dev)]
    each(0, 2, grad_input)
    moves[0].wait()
    summed = acc[:, pl.ds(keep, lanes)] + core_in[...]
    total[...] = summed
    stage[...] = summed.astype(BF16)

    moves = [exchange(stage.at[other_half, :], x_in1, x_dev)]
    moves += [exchange(stage.at[piece2(i), :], z_in2.at[i - 1], z_dev(i)) for i in (2, 1, 3)]
    each(2, 5, grad_input)
    relay(0)
    for moved in moves:
        moved.wait()
    summed = total[own_half, :] + x_in1[...].astype(F32)
    total[own_half, :] = summed
    stage[own_half, :] = summed.astype(BF16)
    summed = total[piece2(0), :]
    for i in range(3):
        summed = summed + z_in2[i].astype(F32)
    total[piece2(0), :] = summed
    stage[piece2(0), :] = summed.astype(BF16)

    moves = [exchange(stage.at[piece1(i), :], z_in1.at[i - 1], z_dev(i)) for i in (2, 1, 3)]
    moves += [exchange(stage.at[quarter2(1 - mx), :], x_in2, x_dev)]
    each(5, CHUNKS, grad_input)
    relay(1)
    for moved in moves:
        moved.wait()
    summed = total[piece1(0), :]
    for i in range(3):
        summed = summed + z_in1[i].astype(F32)
    slots[member, 0:q1, :] = summed.astype(BF16)
    slots[member, q1 : q1 + e2, :] = (total[quarter2(mx), :] + x_in2[...].astype(F32)).astype(BF16)

    moves = [exchange(slots.at[member], slots.at[member], m_dev(i)) for i in range(1, members)]
    relay(2)
    for moved in moves:
        moved.wait()
    summed = slots[0].astype(F32)
    for i in range(1, members):
        summed = summed + slots[i].astype(F32)
    summed = (summed * scale).astype(BF16)
    mine = pl.ds(keep, lanes)
    full[piece1(0), mine] = summed[0:q1]
    full[quarter2(mx), mine] = summed[q1 : q1 + e2]

    def spread(rows, device):
        place = full.at[rows, mine]
        return exchange(place, place, device)

    moves = [spread(piece1(0), z_dev(i)) for i in (2, 1, 3)] + [spread(quarter2(mx), x_dev)]
    relay(3)
    each(HALF, CHUNKS, output)
    for moved in moves:
        moved.wait()
    moves = [spread(own_half, x_dev)] + [spread(piece2(0), z_dev(i)) for i in (2, 1, 3)]
    shared = [spread(own_half, core_dev), spread(piece2(0), core_dev)]
    each(0, HALF, output)
    for moved in moves:
        moved.wait()
    shared += [spread(other_half, core_dev)] + [spread(piece2(i), core_dev) for i in (1, 2, 3)]
    for moved in shared:
        moved.wait()

    @pl.when(frame == 0)
    def _():
        each(0, HALF, lambda i: left(i, rc_sem))
        each(0, HALF, lambda i: left(i, ra_sem))
        each(0, CHUNKS, lambda i: left(i, ay_sem))
        each(0, CHUNKS, lambda i: left(i, az_sem))

    @pl.when(frame == 1)
    def _():
        each(0, CHUNKS, lambda i: left(i, cy_sem))
        each(0, HALF, lambda i: left(i, ay_sem))
        each(0, CHUNKS, lambda i: left(i, az_sem))

    @pl.when(frame == 2)
    def _():
        each(0, CHUNKS, lambda i: left(i, cz_sem))
        each(HALF, CHUNKS, lambda i: left(i, cy_sem))
        each(0, CHUNKS, lambda i: left(i, ay_sem))

    @pl.when(frame == 3)
    def _():
        each(0, CHUNKS, lambda i: left(i, cy_sem))
        each(0, CHUNKS, lambda i: left(i, cz_sem))
        each(HALF, CHUNKS, lambda i: left(i, ra_sem))


def local(frames_in, spatial_weight, temporal_weight, cotangent):
    slab_rows, width, channels = frames_in.shape
    sp_count = lax.axis_size("sp")
    dp_count = lax.axis_size("dp")
    members = sp_count // 4
    cells = slab_rows * width
    size = cells // CHUNKS
    lanes = channels // 2
    x = frames_in.reshape(cells, channels)
    cot = cotangent.reshape(cells, channels)
    w3 = spatial_weight.reshape(3, 3 * channels, channels)
    scale = 1.0 / math.sqrt(slab_rows * sp_count * dp_count * width)

    count = 12 * channels
    h1, q1 = count // 3, count // 12
    q2 = count // 12
    e2 = q2 // 2
    exchanges = 23 + members - 1
    frame = jax.ShapeDtypeStruct((cells, channels), BF16)
    slab = pltpu.VMEM((cells, channels), BF16)
    padded = pltpu.VMEM((cells + 2 * width, 3 * channels), BF16)
    vmem = pl.BlockSpec(memory_space=pltpu.VMEM)
    hbm = pl.BlockSpec(memory_space=pl.ANY)
    block_out, grad_in, grads = pl.pallas_call(
        functools.partial(block_kernel, width, members, scale),
        out_shape=(frame, frame, jax.ShapeDtypeStruct((count, channels), BF16)),
        in_specs=[hbm, hbm, vmem, vmem],
        out_specs=(vmem, vmem, vmem),
        scratch_shapes=[slab] * 7
        + [
            pltpu.VMEM((cells, channels), F32),
            padded,
            padded,
            pltpu.VMEM((3, 3 * channels, channels), BF16),
            pltpu.VMEM((3, channels, channels), BF16),
            pltpu.VMEM((size, channels), F32),
            pltpu.VMEM((count, channels), F32),
            pltpu.VMEM((count, lanes), F32),
            pltpu.VMEM((count, lanes), F32),
            pltpu.VMEM((count, lanes), BF16),
            pltpu.VMEM((h1, lanes), BF16),
            pltpu.VMEM((e2, lanes), BF16),
            pltpu.VMEM((3, q1, lanes), BF16),
            pltpu.VMEM((3, q2, lanes), BF16),
            pltpu.VMEM((members, q1 + e2, lanes), BF16),
            pltpu.SemaphoreType.DMA((2,)),
        ]
        + [pltpu.SemaphoreType.DMA((CHUNKS,))] * 10
        + [pltpu.SemaphoreType.DMA((exchanges,))] * 2,
        compiler_params=pltpu.CompilerParams(
            collective_id=0, has_side_effects=True, vmem_limit_bytes=VMEM_LIMIT
        ),
        cost_estimate=pl.CostEstimate(
            flops=72 * cells * channels * channels,
            bytes_accessed=16 * cells * channels,
            transcendentals=2 * cells * channels,
        ),
        name="video_block",
    )(x, cot, w3, temporal_weight)

    grads = grads.astype(F32)
    grad_spatial = grads[: 9 * channels].reshape(3, 3, channels, channels)
    grad_temporal = grads[9 * channels :].reshape(3, channels, channels)
    return (
        block_out.reshape(frames_in.shape),
        grad_in.reshape(frames_in.shape),
        grad_spatial,
        grad_temporal,
    )


def solution(mesh):
    placed = (P(("dp", "sp"), None, None), P(), P(), P(("dp", "sp"), None, None))
    return jax.shard_map(
        local,
        mesh=mesh,
        in_specs=placed,
        out_specs=(P(("dp", "sp"), None, None), P(("dp", "sp"), None, None), P(), P()),
        check_vma=False,
    )
```

```python
import functools
import math

import jax
import jax.numpy as jnp
from jax import lax
from jax.experimental import pallas as pl
from jax.experimental.pallas import tpu as pltpu
from jax.sharding import PartitionSpec as P

FRAMES = 4
CHUNKS = 8
HALF = CHUNKS // 2
LEAD = CHUNKS // 8
VIA = 2
HOLD = 1
HELD_AT = (19.3,)
GRAD_INPUT_AT = ((1, 3.0), (0, 3.1))
RELAY_AT = (2.5, 13.5)
LAST_AT = (19.5, 19.6)
OUTPUT_AT = ((20.5, 4, 5), (20.6, 5, 6), (22.5, 6, 7), (28.0, 0, 2), (28.1, 7, 8), (28.2, 3, 4), (28.3, 2, 3))
VMEM_LIMIT = 58 * 1024 * 1024
MESH = pl.DeviceIdType.MESH
F32 = jnp.float32
BF16 = jnp.bfloat16


def mm(left, right):
    return jnp.dot(left, right, preferred_element_type=F32)


def store_shifted(dest, offset, values, width):
    cells, channels = values.shape
    column = lax.broadcasted_iota(jnp.int32, (cells, channels), 0) % width
    before = jnp.where(column == 0, 0.0, pltpu.roll(values, 1, axis=0))
    after = jnp.where(column == width - 1, 0.0, pltpu.roll(values, cells - 1, axis=0))
    dest[pl.ds(offset, cells), 0:channels] = before.astype(BF16)
    dest[pl.ds(offset, cells), channels : 2 * channels] = values.astype(BF16)
    dest[pl.ds(offset, cells), 2 * channels : 3 * channels] = after.astype(BF16)


def zero_edges(dest, width):
    rows, lanes = dest.shape
    dest[0:width] = jnp.zeros((width, lanes), BF16)
    dest[rows - width : rows] = jnp.zeros((width, lanes), BF16)


def block_kernel(
    width, members, scale,
    x_hbm, cot_hbm, w_ref, tw_ref,
    out_hbm, gin_hbm, full,
    x, cot, c1, c2, a1, a2, act, out, gin, slope, x3, g3, wf, wt, part, acc,
    core_in, total, stage, x_in, z_in, slots,
    load_sem, c1_sem, c2_sem, a1_sem, a2_sem, cy_sem, cz_sem, ay_sem, az_sem, rc_sem, ra_sem,
    out_sem, gin_sem, red_send, red_recv,
):
    dp = lax.axis_index("dp")
    sp = lax.axis_index("sp")
    frame = sp % FRAMES
    y = sp % 2
    zi = (sp // 2) % 4
    group = sp // 8
    member = y + 2 * group
    core = dp % 2
    mx = (dp // 2) % 2
    cells, channels = x.shape
    size = cells // CHUNKS
    lanes = channels // 2

    y_dev = (dp, sp + 1 - 2 * y)
    t_dev = (dp, sp + 2 - 4 * (zi % 2))
    core_dev = (dp + 1 - 2 * core, sp)
    x_dev = (dp + 2 - 4 * mx, sp)

    def z_member(offset):
        return (zi + offset) % 4

    def z_dev(offset):
        return (dp, sp + (z_member(offset) - zi) * 2)

    def m_dev(offset):
        other = (member + offset) % members
        return (dp, sp + other % 2 - y + (other // 2 - group) * 8)

    def chunk(ref, index):
        return ref.at[pl.ds(pl.multiple_of(index * size, size), size), :]

    def copy(source, dest, send_sem, recv_sem, device):
        return pltpu.make_async_remote_copy(
            src_ref=source, dst_ref=dest, send_sem=send_sem, recv_sem=recv_sem,
            device_id=device, device_id_type=MESH,
        )

    def send(source, dest, index, send_sems, recv_sems, device):
        copy(
            chunk(source, index), chunk(dest, index), send_sems.at[index], recv_sems.at[index], device
        ).start()

    def arrived(dest, index, recv_sems):
        copy(
            chunk(dest, index), chunk(dest, index), recv_sems.at[index], recv_sems.at[index], y_dev
        ).wait_recv()

    def left(index, send_sems):
        copy(
            chunk(act, index), chunk(act, index), send_sems.at[index], send_sems.at[index], y_dev
        ).wait_send()

    def each(start, stop, body):
        def step(index, carry):
            body(index)
            return carry

        lax.fori_loop(start, stop, step, 0)

    x_load = pltpu.make_async_copy(x_hbm, x, load_sem.at[0])
    cot_load = pltpu.make_async_copy(cot_hbm, cot, load_sem.at[1])
    x_load.start()
    cot_load.start()

    barrier = pltpu.get_barrier_semaphore()
    greeted = [core_dev, x_dev] + [z_dev(i) for i in (1, 2, 3)] + [m_dev(i) for i in range(1, members)]
    for device in greeted:
        pl.semaphore_signal(barrier, inc=1, device_id=device, device_id_type=MESH)
    pl.semaphore_wait(barrier, len(greeted))

    @pl.when(frame == 1)
    def _():
        each(0, CHUNKS, lambda i: send(cot_hbm, c1, i, cy_sem, c1_sem, y_dev))

    @pl.when(frame == 2)
    def _():
        each(0, CHUNKS, lambda i: send(cot_hbm, c2, i, cz_sem, c2_sem, t_dev))
        each(HALF, CHUNKS, lambda i: send(cot_hbm, c1, i, cy_sem, c1_sem, y_dev))

    @pl.when(frame == 3)
    def _():
        each(0, CHUNKS, lambda i: send(cot_hbm, c1, i, cy_sem, c1_sem, y_dev))
        each(0, HALF, lambda i: send(cot_hbm, c2, i, cz_sem, c2_sem, t_dev))

    acc[...] = jnp.zeros_like(acc)
    zero_edges(x3, width)
    zero_edges(g3, width)
    x_load.wait()

    def forward(step):
        @pl.when(step < CHUNKS)
        def _():
            store_shifted(
                x3, pl.multiple_of(width + step * size, width),
                x[pl.ds(pl.multiple_of(step * size, size), size), :].astype(F32), width,
            )

        @pl.when(step >= 1)
        def _():
            index = step - 1
            base = pl.multiple_of(index * size, size)
            pre = jnp.zeros((size, channels), F32)
            for tap in range(3):
                pre = pre + mm(x3[pl.ds(base + tap * width, size), :], w_ref[tap])
            sigma = jax.nn.sigmoid(pre)
            act[pl.ds(base, size), :] = (pre * sigma).astype(BF16)
            slope[pl.ds(base, size), :] = sigma * (1.0 + pre * (1.0 - sigma))

            @pl.when(frame == 0)
            def _():
                send(act, a2, index, az_sem, a2_sem, t_dev)

            @pl.when((frame == 0) & (index < LEAD))
            def _():
                send(act, a1, index, ay_sem, a1_sem, y_dev)

            @pl.when((frame == 1) & (index < VIA))
            def _():
                send(act, a1, index, ay_sem, a1_sem, y_dev)

            @pl.when((frame == 1) & (index >= HALF))
            def _():
                send(act, a2, index, az_sem, a2_sem, t_dev)

            @pl.when((frame == 2) & (index < CHUNKS - HOLD))
            def _():
                send(act, a1, index, ay_sem, a1_sem, y_dev)

    each(0, CHUNKS + 1, forward)

    @pl.when(frame == 1)
    def _():
        each(0, HALF, lambda i: send(act, a2, HALF - 1 - i, az_sem, a2_sem, t_dev))

    for tap in range(3):
        wt[tap] = tw_ref[tap].T
        for side in range(3):
            wf[tap, side * channels : (side + 1) * channels, :] = w_ref[
                2 - tap, (2 - side) * channels : (3 - side) * channels, :
            ].T
    cot_load.wait()

    gt_base = 9 * channels
    block = 3 * channels

    def add_temporal(tap, act_t, other):
        acc[gt_base + tap * channels : gt_base + (tap + 1) * channels, :] += mm(act_t, other)

    def receive(index):
        rows = pl.ds(pl.multiple_of(index * size, size), size)
        early = index < HALF

        @pl.when((frame < 3) | (index >= HALF))
        def _():
            arrived(c1, index, c1_sem)

        @pl.when((frame == 0) | ((frame == 1) & early))
        def _():
            arrived(c2, index, c2_sem)

        @pl.when((frame == 0) & early)
        def _():
            send(c2, c1, index, rc_sem, c1_sem, y_dev)

        @pl.when((frame == 0) & (index == HALF - 1))
        def _():
            each(LEAD, CHUNKS - HOLD, lambda i: send(act, a1, i, ay_sem, a1_sem, y_dev))

        @pl.when((frame == 3) & (index >= HALF))
        def _():
            c2[rows, :] = (mm(c1[rows, :], wt[1]) + mm(cot[rows, :], wt[2])).astype(BF16)
            send(c2, c1, index, cz_sem, c1_sem, t_dev)

    def backward(index, finish):
        base = pl.multiple_of(index * size, size)
        rows = pl.ds(base, size)
        early = index < HALF
        act_t = act[rows, :].T
        part[...] = mm(cot[rows, :], wt[0])
        add_temporal(0, act_t, cot[rows, :])

        @pl.when((frame == 0) | (frame == 2) | ((frame == 1) & early))
        def _():
            part[...] += mm(c1[rows, :], wt[1])
            add_temporal(1, act_t, c1[rows, :])

        @pl.when((frame == 0) | ((frame == 1) & early))
        def _():
            part[...] += mm(c2[rows, :], wt[2])
            add_temporal(2, act_t, c2[rows, :])

        finish(0)

        @pl.when((frame == 1) & (index >= HALF))
        def _():
            part[...] += c1[rows, :].astype(F32)

        grad_pre = part[...].astype(BF16).astype(F32) * slope[rows, :]
        store_shifted(g3, pl.multiple_of(width + base, width), grad_pre, width)
        grad_pre = grad_pre.astype(BF16)
        for tap in range(3):
            window = x3[pl.ds(base + tap * width, size), :]
            acc[tap * block : (tap + 1) * block, :] += mm(window.T, grad_pre)
            finish(1 + tap)

    def grad_input(index):
        base = pl.multiple_of(index * size, size)
        total_in = cot[pl.ds(base, size), :].astype(F32)
        for tap in range(3):
            total_in = total_in + mm(g3[pl.ds(base + tap * width, size), :], wf[tap])
        gin[pl.ds(base, size), :] = total_in.astype(BF16)
        pltpu.make_async_copy(chunk(gin, index), chunk(gin_hbm, index), gin_sem.at[index]).start()

    def output(index):
        rows = pl.ds(pl.multiple_of(index * size, size), size)

        @pl.when(frame >= 1)
        def _():
            arrived(a1, index, a1_sem)

        @pl.when((frame == 2) | ((frame == 3) & (index < VIA)))
        def _():
            arrived(a2, index, a2_sem)

        part[...] = mm(act[rows, :], tw_ref[0])

        @pl.when(frame >= 1)
        def _():
            part[...] += mm(a1[rows, :], tw_ref[1])

        @pl.when(frame >= 2)
        def _():
            part[...] += mm(a2[rows, :], tw_ref[2])

        temporal = part[...].astype(BF16).astype(F32)
        out[rows, :] = (x[rows, :].astype(F32) + temporal).astype(BF16)
        pltpu.make_async_copy(chunk(out, index), chunk(out_hbm, index), out_sem.at[index]).start()

    def relay_first(index):
        @pl.when(frame == 0)
        def _():
            arrived(a1, index, a1_sem)
            send(a1, a1, index, ra_sem, a1_sem, t_dev)

    def relay_last(index):
        @pl.when(frame == 3)
        def _():
            arrived(a2, index, a2_sem)
            send(a2, a1, index, ra_sem, a1_sem, y_dev)

    def held(index):
        @pl.when((frame == 0) | (frame == 2))
        def _():
            send(act, a1, index, ay_sem, a1_sem, y_dev)

    half, piece = block // 2, block // 8
    keep = pl.multiple_of(core * lanes, lanes)
    give = pl.multiple_of((1 - core) * lanes, lanes)
    mine = pl.ds(keep, lanes)
    bases = [gt_base] + [tap * block for tap in range(3)]
    used = []
    moving = {}

    def exchange(name, source, dest, device):
        slot = len(used)
        used.append(slot)
        moved = copy(source, dest, red_send.at[slot], red_recv.at[slot], device)
        moved.start()
        moving.setdefault(name, []).append(moved)

    def landed(name):
        for moved in moving.pop(name):
            moved.wait()

    def rows_of(start, length):
        return pl.ds(pl.multiple_of(start, 16), length)

    def half_of(which, part_x):
        return rows_of(bases[which] + part_x * half, half)

    def piece_of(which, offset):
        return rows_of(bases[which] + mx * half + z_member(offset) * piece, piece)

    def spread(name, rows, device):
        place = full.at[rows, mine]
        exchange(name, place, place, device)

    def to_core(which):
        rows = rows_of(bases[which], block)
        exchange(("core", which), acc.at[rows, pl.ds(give, lanes)], core_in.at[rows, :], core_dev)

    def to_x(which):
        landed(("core", which))
        rows = rows_of(bases[which], block)
        summed = acc[rows, mine] + core_in[rows, :]
        total[rows, :] = summed
        stage[rows, :] = summed.astype(BF16)
        exchange(("x", which), stage.at[half_of(which, 1 - mx), :], x_in.at[which], x_dev)

    def to_z(which):
        landed(("x", which))
        rows = half_of(which, mx)
        summed = total[rows, :] + x_in[which].astype(F32)
        total[rows, :] = summed
        stage[rows, :] = summed.astype(BF16)
        for offset in (2, 1, 3):
            exchange(
                ("z", which), stage.at[piece_of(which, offset), :], z_in.at[which, offset - 1],
                z_dev(offset),
            )

    def to_y(which):
        landed(("z", which))
        summed = total[piece_of(which, 0), :]
        for offset in range(3):
            summed = summed + z_in[which, offset].astype(F32)
        slots[which, member] = summed.astype(BF16)
        place = slots.at[which, member]
        for offset in range(1, members):
            exchange(("y", which), place, place, m_dev(offset))

    def back_z(which):
        landed(("y", which))
        summed = slots[which, 0].astype(F32)
        for other in range(1, members):
            summed = summed + slots[which, other].astype(F32)
        full[piece_of(which, 0), mine] = (summed * scale).astype(BF16)
        for offset in (2, 1, 3):
            spread(("backz", which), piece_of(which, 0), z_dev(offset))
        spread(("backx", which), piece_of(which, 0), x_dev)

    def back_x(which):
        landed(("backz", which))
        for offset in (2, 3, 1):
            spread(("backx", which), piece_of(which, offset), x_dev)
        spread(("last", which), half_of(which, mx), core_dev)

    def back_core(which):
        landed(("backx", which))
        spread(("last", which), half_of(which, 1 - mx), core_dev)

    def fill_in(index):
        receive(index)
        backward(index, lambda which: None)

        @pl.when(index >= 1)
        def _():
            grad_input(index - 1)

    each(0, CHUNKS - 1, fill_in)
    receive(CHUNKS - 1)

    @pl.when(frame == 3)
    def _():
        def late(index):
            rows = pl.ds(pl.multiple_of(index * size, size), size)
            relay_last(index)
            act_t = a2[rows, :].T
            add_temporal(1, act_t, c1[rows, :])
            add_temporal(2, act_t, cot[rows, :])

        each(HALF, CHUNKS, late)

    backward(CHUNKS - 1, to_core)

    later = []
    for which in range(4):
        later += [
            (0.5 + 0.6 * which, to_x, which), (5.6 + 2.1 * which, to_z, which),
            (10.0 + 2.1 * which, to_y, which), (12.8 + 2.1 * which, back_z, which),
            (17.2 + 2.1 * which, back_x, which), (20.0 + 2.1 * which, back_core, which),
        ]
    for index, when in GRAD_INPUT_AT:
        later.append((when, grad_input, CHUNKS - 1 - index))
    for index, when in enumerate(RELAY_AT):
        later.append((when, relay_first, index))
    for index, when in enumerate(LAST_AT):
        later.append((when, relay_last, HALF - 1 - index))
    for index, when in enumerate(HELD_AT):
        later.append((when, held, CHUNKS - HOLD + index))
    for when, start, stop in OUTPUT_AT:
        later.append((when, lambda span: each(span[0], span[1], output), (start, stop)))
    for _, action, argument in sorted(later, key=lambda entry: entry[0]):
        action(argument)
    for which in range(4):
        landed(("last", which))

    def written(index):
        pltpu.make_async_copy(chunk(gin, index), chunk(gin_hbm, index), gin_sem.at[index]).wait()
        pltpu.make_async_copy(chunk(out, index), chunk(out_hbm, index), out_sem.at[index]).wait()

    each(0, CHUNKS, written)

    @pl.when(frame == 0)
    def _():
        each(0, HALF, lambda i: left(i, rc_sem))
        each(0, VIA, lambda i: left(i, ra_sem))
        each(0, CHUNKS, lambda i: left(i, ay_sem))
        each(0, CHUNKS, lambda i: left(i, az_sem))

    @pl.when(frame == 1)
    def _():
        each(0, CHUNKS, lambda i: left(i, cy_sem))
        each(0, VIA, lambda i: left(i, ay_sem))
        each(0, CHUNKS, lambda i: left(i, az_sem))

    @pl.when(frame == 2)
    def _():
        each(0, CHUNKS, lambda i: left(i, cz_sem))
        each(HALF, CHUNKS, lambda i: left(i, cy_sem))
        each(0, CHUNKS, lambda i: left(i, ay_sem))

    @pl.when(frame == 3)
    def _():
        each(0, CHUNKS, lambda i: left(i, cy_sem))
        each(0, CHUNKS, lambda i: left(i, cz_sem))
        each(VIA, CHUNKS, lambda i: left(i, ra_sem))


def finish_kernel(
    out_in, gin_in, grads_in, out_hbm, gin_hbm, spatial_hbm, temporal_hbm,
    out, gin, grads, wide, in_sem, out_sem,
):
    rows = out.shape[0] // 4
    block = grads.shape[0] // 4
    loads, stores = [], []

    def start(moves, source, dest, sems):
        moves.append(pltpu.make_async_copy(source, dest, sems.at[len(moves)]))
        moves[-1].start()

    parts = [pl.ds(part * block, block) for part in range(4)]
    slabs = [pl.ds(part * rows, rows) for part in range(4)]
    for part in parts:
        start(loads, grads_in.at[part, :], grads.at[part, :], in_sem)
    for source, dest in ((out_in, out), (gin_in, gin)):
        for slab in slabs:
            start(loads, source.at[slab, :], dest.at[slab, :], in_sem)
    for index, part in enumerate(parts):
        loads[index].wait()
        wide[part, :] = grads[part, :].astype(F32)
        target = spatial_hbm.at[part, :] if index < 3 else temporal_hbm
        start(stores, wide.at[part, :], target, out_sem)
    index = 4
    for source, dest in ((out, out_hbm), (gin, gin_hbm)):
        for slab in slabs:
            loads[index].wait()
            index += 1
            start(stores, source.at[slab, :], dest.at[slab, :], out_sem)
    for move in stores:
        move.wait()


def local(frames_in, spatial_weight, temporal_weight, cotangent):
    slab_rows, width, channels = frames_in.shape
    sp_count = lax.axis_size("sp")
    dp_count = lax.axis_size("dp")
    members = sp_count // 4
    cells = slab_rows * width
    size = cells // CHUNKS
    lanes = channels // 2
    x = frames_in.reshape(cells, channels)
    cot = cotangent.reshape(cells, channels)
    w3 = spatial_weight.reshape(3, 3 * channels, channels)
    scale = 1.0 / math.sqrt(slab_rows * sp_count * dp_count * width)

    count = 12 * channels
    block = 3 * channels
    half, piece = block // 2, block // 8
    exchanges = 4 * (14 + members - 1)
    frame = jax.ShapeDtypeStruct((cells, channels), BF16)
    slab = pltpu.VMEM((cells, channels), BF16)
    padded = pltpu.VMEM((cells + 2 * width, 3 * channels), BF16)
    vmem = pl.BlockSpec(memory_space=pltpu.VMEM)
    hbm = pl.BlockSpec(memory_space=pl.ANY)
    block_out, grad_in, grads = pl.pallas_call(
        functools.partial(block_kernel, width, members, scale),
        out_shape=(frame, frame, jax.ShapeDtypeStruct((count, channels), BF16)),
        in_specs=[hbm, hbm, vmem, vmem],
        out_specs=(hbm, hbm, vmem),
        scratch_shapes=[slab] * 9
        + [
            pltpu.VMEM((cells, channels), F32),
            padded,
            padded,
            pltpu.VMEM((3, block, channels), BF16),
            pltpu.VMEM((3, channels, channels), BF16),
            pltpu.VMEM((size, channels), F32),
            pltpu.VMEM((count, channels), F32),
            pltpu.VMEM((count, lanes), F32),
            pltpu.VMEM((count, lanes), F32),
            pltpu.VMEM((count, lanes), BF16),
            pltpu.VMEM((4, half, lanes), BF16),
            pltpu.VMEM((4, 3, piece, lanes), BF16),
            pltpu.VMEM((4, members, piece, lanes), BF16),
            pltpu.SemaphoreType.DMA((2,)),
        ]
        + [pltpu.SemaphoreType.DMA((CHUNKS,))] * 12
        + [pltpu.SemaphoreType.DMA((exchanges,))] * 2,
        compiler_params=pltpu.CompilerParams(
            collective_id=0, has_side_effects=True, vmem_limit_bytes=VMEM_LIMIT
        ),
        cost_estimate=pl.CostEstimate(
            flops=72 * cells * channels * channels,
            bytes_accessed=16 * cells * channels,
            transcendentals=2 * cells * channels,
        ),
        name="video_block",
    )(x, cot, w3, temporal_weight)

    block_out, grad_in, grad_spatial, grad_temporal = pl.pallas_call(
        finish_kernel,
        out_shape=(
            frame, frame,
            jax.ShapeDtypeStruct((9 * channels, channels), F32),
            jax.ShapeDtypeStruct((3 * channels, channels), F32),
        ),
        in_specs=[hbm] * 3,
        out_specs=(hbm,) * 4,
        scratch_shapes=[
            slab,
            slab,
            pltpu.VMEM((count, channels), BF16),
            pltpu.VMEM((count, channels), F32),
            pltpu.SemaphoreType.DMA((12,)),
            pltpu.SemaphoreType.DMA((12,)),
        ],
        compiler_params=pltpu.CompilerParams(vmem_limit_bytes=VMEM_LIMIT),
        name="finish",
    )(block_out, grad_in, grads)
    grad_spatial = grad_spatial.reshape(3, 3, channels, channels)
    grad_temporal = grad_temporal.reshape(3, channels, channels)
    return (
        block_out.reshape(frames_in.shape),
        grad_in.reshape(frames_in.shape),
        grad_spatial,
        grad_temporal,
    )


def solution(mesh):
    placed = (P(("dp", "sp"), None, None), P(), P(), P(("dp", "sp"), None, None))
    return jax.shard_map(
        local,
        mesh=mesh,
        in_specs=placed,
        out_specs=(P(("dp", "sp"), None, None), P(("dp", "sp"), None, None), P(), P()),
        check_vma=False,
    )
```

```python
import functools
import math

import jax
import jax.numpy as jnp
from jax import lax
from jax.experimental import pallas as pl
from jax.experimental.pallas import tpu as pltpu
from jax.sharding import PartitionSpec as P

FRAMES = 4
CHUNKS = 8
HALF = CHUNKS // 2
LEAD = CHUNKS // 8
VIA = 2
HOLD = 1
Z_FIRST = (0,)
SPLIT = 1
X_FIRST_AT = ((0.5, 0.6), (3.5, 2.1), (8.0, 2.1), (10.8, 2.1), (15.2, 2.1), (18.0, 2.1))
Z_FIRST_AT = ((0.5, 0.6), (8.0, 0.6), (11.0, 0.6), (13.8, 0.6), (18.3, 2.1), (20.9, 2.1))
HELD_AT = (19.3,)
GRAD_INPUT_AT = ((1, 3.0), (0, 3.1))
RELAY_AT = (2.5, 13.5)
LAST_AT = (14.5, 19.6)
OUTPUT_AT = ((20.5, 4, 5), (20.6, 5, 6), (22.5, 6, 7), (28.0, 0, 2), (28.1, 7, 8), (28.2, 3, 4), (28.3, 2, 3))
VMEM_LIMIT = 48 * 1024 * 1024
MESH = pl.DeviceIdType.MESH
F32 = jnp.float32
BF16 = jnp.bfloat16


def mm(left, right):
    return jnp.dot(left, right, preferred_element_type=F32)


def store_shifted(dest, offset, values, width):
    cells, channels = values.shape
    column = lax.broadcasted_iota(jnp.int32, (cells, channels), 0) % width
    before = jnp.where(column == 0, 0.0, pltpu.roll(values, 1, axis=0))
    after = jnp.where(column == width - 1, 0.0, pltpu.roll(values, cells - 1, axis=0))
    dest[pl.ds(offset, cells), 0:channels] = before.astype(BF16)
    dest[pl.ds(offset, cells), channels : 2 * channels] = values.astype(BF16)
    dest[pl.ds(offset, cells), 2 * channels : 3 * channels] = after.astype(BF16)


def zero_edges(dest, width):
    rows, lanes = dest.shape
    dest[0:width] = jnp.zeros((width, lanes), BF16)
    dest[rows - width : rows] = jnp.zeros((width, lanes), BF16)


def block_kernel(
    width, members, scale,
    x_hbm, cot_hbm, w_hbm, tw_hbm,
    out, gin, full,
    x, cot, c1, c2, a1, a2, act, slope, x3, g3, w_ref, tw_ref, wf, wt, part, acc,
    core_in, total, stage, x_in, z_in, slots,
    load_sem, c1_sem, c2_sem, a1_sem, a2_sem, cy_sem, cz_sem, ay_sem, az_sem, rc_sem, ra_sem,
    red_send, red_recv,
):
    dp = lax.axis_index("dp")
    sp = lax.axis_index("sp")
    frame = sp % FRAMES
    y = sp % 2
    zi = (sp // 2) % 4
    group = sp // 8
    member = y + 2 * group
    core = dp % 2
    mx = (dp // 2) % 2
    cells, channels = x.shape
    size = cells // CHUNKS
    lanes = channels // 2

    y_dev = (dp, sp + 1 - 2 * y)
    t_dev = (dp, sp + 2 - 4 * (zi % 2))
    core_dev = (dp + 1 - 2 * core, sp)
    x_dev = (dp + 2 - 4 * mx, sp)

    def z_member(offset):
        return (zi + offset) % 4

    def z_dev(offset):
        return (dp, sp + (z_member(offset) - zi) * 2)

    def m_dev(offset):
        other = (member + offset) % members
        return (dp, sp + other % 2 - y + (other // 2 - group) * 8)

    def chunk(ref, index):
        return ref.at[pl.ds(pl.multiple_of(index * size, size), size), :]

    def copy(source, dest, send_sem, recv_sem, device):
        return pltpu.make_async_remote_copy(
            src_ref=source, dst_ref=dest, send_sem=send_sem, recv_sem=recv_sem,
            device_id=device, device_id_type=MESH,
        )

    def send(source, dest, index, send_sems, recv_sems, device):
        copy(
            chunk(source, index), chunk(dest, index), send_sems.at[index], recv_sems.at[index], device
        ).start()

    def arrived(dest, index, recv_sems):
        copy(
            chunk(dest, index), chunk(dest, index), recv_sems.at[index], recv_sems.at[index], y_dev
        ).wait_recv()

    def left(index, send_sems):
        copy(
            chunk(act, index), chunk(act, index), send_sems.at[index], send_sems.at[index], y_dev
        ).wait_send()

    def each(start, stop, body):
        def step(index, carry):
            body(index)
            return carry

        lax.fori_loop(start, stop, step, 0)

    x_load = pltpu.make_async_copy(x_hbm, x, load_sem.at[0])
    cot_load = pltpu.make_async_copy(cot_hbm, cot, load_sem.at[1])
    w_load = pltpu.make_async_copy(w_hbm, w_ref, load_sem.at[2])
    tw_load = pltpu.make_async_copy(tw_hbm, tw_ref, load_sem.at[3])
    for load in (x_load, w_load, tw_load, cot_load):
        load.start()

    barrier = pltpu.get_barrier_semaphore()
    greeted = [core_dev, x_dev] + [z_dev(i) for i in (1, 2, 3)] + [m_dev(i) for i in range(1, members)]
    for device in greeted:
        pl.semaphore_signal(barrier, inc=1, device_id=device, device_id_type=MESH)
    pl.semaphore_wait(barrier, len(greeted))

    @pl.when(frame == 1)
    def _():
        each(0, CHUNKS, lambda i: send(cot_hbm, c1, i, cy_sem, c1_sem, y_dev))

    @pl.when(frame == 2)
    def _():
        each(0, CHUNKS, lambda i: send(cot_hbm, c2, i, cz_sem, c2_sem, t_dev))
        each(HALF, CHUNKS, lambda i: send(cot_hbm, c1, i, cy_sem, c1_sem, y_dev))

    @pl.when(frame == 3)
    def _():
        each(0, CHUNKS, lambda i: send(cot_hbm, c1, i, cy_sem, c1_sem, y_dev))
        each(0, HALF, lambda i: send(cot_hbm, c2, i, cz_sem, c2_sem, t_dev))

    acc[...] = jnp.zeros_like(acc)
    zero_edges(x3, width)
    zero_edges(g3, width)
    x_load.wait()
    w_load.wait()

    def forward(step):
        @pl.when(step < CHUNKS)
        def _():
            store_shifted(
                x3, pl.multiple_of(width + step * size, width),
                x[pl.ds(pl.multiple_of(step * size, size), size), :].astype(F32), width,
            )

        @pl.when(step >= 1)
        def _():
            index = step - 1
            base = pl.multiple_of(index * size, size)
            pre = jnp.zeros((size, channels), F32)
            for tap in range(3):
                pre = pre + mm(x3[pl.ds(base + tap * width, size), :], w_ref[tap])
            sigma = jax.nn.sigmoid(pre)
            act[pl.ds(base, size), :] = (pre * sigma).astype(BF16)
            slope[pl.ds(base, size), :] = sigma * (1.0 + pre * (1.0 - sigma))

            @pl.when(frame == 0)
            def _():
                send(act, a2, index, az_sem, a2_sem, t_dev)

            @pl.when((frame == 0) & (index < LEAD))
            def _():
                send(act, a1, index, ay_sem, a1_sem, y_dev)

            @pl.when((frame == 1) & (index < VIA))
            def _():
                send(act, a1, index, ay_sem, a1_sem, y_dev)

            @pl.when((frame == 1) & (index >= HALF))
            def _():
                send(act, a2, index, az_sem, a2_sem, t_dev)

            @pl.when((frame == 2) & (index < CHUNKS - HOLD))
            def _():
                send(act, a1, index, ay_sem, a1_sem, y_dev)

    each(0, CHUNKS + 1, forward)

    @pl.when(frame == 1)
    def _():
        each(0, HALF, lambda i: send(act, a2, HALF - 1 - i, az_sem, a2_sem, t_dev))

    tw_load.wait()
    for tap in range(3):
        wt[tap] = tw_ref[tap].T
        for side in range(3):
            wf[tap, side * channels : (side + 1) * channels, :] = w_ref[
                2 - tap, (2 - side) * channels : (3 - side) * channels, :
            ].T
    cot_load.wait()

    gt_base = 9 * channels
    block = 3 * channels

    def add_temporal(tap, act_t, other):
        acc[gt_base + tap * channels : gt_base + (tap + 1) * channels, :] += mm(act_t, other)

    def receive(index):
        rows = pl.ds(pl.multiple_of(index * size, size), size)
        early = index < HALF

        @pl.when((frame < 3) | (index >= HALF))
        def _():
            arrived(c1, index, c1_sem)

        @pl.when((frame == 0) | ((frame == 1) & early))
        def _():
            arrived(c2, index, c2_sem)

        @pl.when((frame == 0) & early)
        def _():
            send(c2, c1, index, rc_sem, c1_sem, y_dev)

        @pl.when((frame == 0) & (index == HALF - 1))
        def _():
            each(LEAD, CHUNKS - HOLD, lambda i: send(act, a1, i, ay_sem, a1_sem, y_dev))

        @pl.when((frame == 3) & (index >= HALF))
        def _():
            c2[rows, :] = (mm(c1[rows, :], wt[1]) + mm(cot[rows, :], wt[2])).astype(BF16)
            send(c2, c1, index, cz_sem, c1_sem, t_dev)

    def backward(index, finish):
        base = pl.multiple_of(index * size, size)
        rows = pl.ds(base, size)
        early = index < HALF
        act_t = act[rows, :].T
        part[...] = mm(cot[rows, :], wt[0])
        add_temporal(0, act_t, cot[rows, :])

        @pl.when((frame == 0) | (frame == 2) | ((frame == 1) & early))
        def _():
            part[...] += mm(c1[rows, :], wt[1])
            add_temporal(1, act_t, c1[rows, :])

        @pl.when((frame == 0) | ((frame == 1) & early))
        def _():
            part[...] += mm(c2[rows, :], wt[2])
            add_temporal(2, act_t, c2[rows, :])

        finish(0)

        @pl.when((frame == 1) & (index >= HALF))
        def _():
            part[...] += c1[rows, :].astype(F32)

        grad_pre = part[...].astype(BF16).astype(F32) * slope[rows, :]
        store_shifted(g3, pl.multiple_of(width + base, width), grad_pre, width)
        grad_pre = grad_pre.astype(BF16)
        for tap in range(3):
            window = x3[pl.ds(base + tap * width, size), :]
            acc[tap * block : (tap + 1) * block, :] += mm(window.T, grad_pre)
            finish(1 + tap)

    def grad_input(index):
        base = pl.multiple_of(index * size, size)
        total_in = cot[pl.ds(base, size), :].astype(F32)
        for tap in range(3):
            total_in = total_in + mm(g3[pl.ds(base + tap * width, size), :], wf[tap])
        gin[pl.ds(base, size), :] = total_in.astype(BF16)

    def output(index):
        rows = pl.ds(pl.multiple_of(index * size, size), size)

        @pl.when(frame >= 1)
        def _():
            arrived(a1, index, a1_sem)

        @pl.when((frame == 2) | ((frame == 3) & (index < VIA)))
        def _():
            arrived(a2, index, a2_sem)

        part[...] = mm(act[rows, :], tw_ref[0])

        @pl.when(frame >= 1)
        def _():
            part[...] += mm(a1[rows, :], tw_ref[1])

        @pl.when(frame >= 2)
        def _():
            part[...] += mm(a2[rows, :], tw_ref[2])

        temporal = part[...].astype(BF16).astype(F32)
        out[rows, :] = (x[rows, :].astype(F32) + temporal).astype(BF16)

    def relay_first(index):
        @pl.when(frame == 0)
        def _():
            arrived(a1, index, a1_sem)
            send(a1, a1, index, ra_sem, a1_sem, t_dev)

    def relay_last(index):
        @pl.when(frame == 3)
        def _():
            arrived(a2, index, a2_sem)
            send(a2, a1, index, ra_sem, a1_sem, y_dev)

    def held(index):
        @pl.when((frame == 0) | (frame == 2))
        def _():
            send(act, a1, index, ay_sem, a1_sem, y_dev)

    span = block // SPLIT
    half, piece = span // 2, span // 8
    keep = pl.multiple_of(core * lanes, lanes)
    give = pl.multiple_of((1 - core) * lanes, lanes)
    mine = pl.ds(keep, lanes)
    bases = [
        start + part_of * span
        for start in [gt_base] + [tap * block for tap in range(3)]
        for part_of in range(SPLIT)
    ]
    used = []
    moving = {}

    def exchange(name, source, dest, device):
        slot = len(used)
        used.append(slot)
        moved = copy(source, dest, red_send.at[slot], red_recv.at[slot], device)
        moved.start()
        moving.setdefault(name, []).append(moved)

    def landed(name):
        for moved in moving.pop(name):
            moved.wait()

    def rows_of(start, length):
        return pl.ds(pl.multiple_of(start, 16), length)

    def half_of(which, part_x):
        return rows_of(bases[which] + part_x * half, half)

    def piece_of(which, offset):
        if which in Z_FIRST:
            return rows_of(bases[which] + z_member(offset) * 2 * piece + mx * piece, piece)
        return rows_of(bases[which] + mx * half + z_member(offset) * piece, piece)

    def pair_of(which, offset):
        return rows_of(bases[which] + z_member(offset) * 2 * piece, 2 * piece)

    def spread(name, rows, device):
        place = full.at[rows, mine]
        exchange(name, place, place, device)

    def to_core(which):
        rows = rows_of(bases[which], span)
        exchange(("core", which), acc.at[rows, pl.ds(give, lanes)], core_in.at[rows, :], core_dev)

    def to_first(which):
        landed(("core", which))
        rows = rows_of(bases[which], span)
        summed = acc[rows, mine] + core_in[rows, :]
        total[rows, :] = summed
        stage[rows, :] = summed.astype(BF16)
        if which in Z_FIRST:
            for offset in (2, 1, 3):
                exchange(
                    ("first", which), stage.at[pair_of(which, offset), :],
                    z_in.at[which, offset - 1], z_dev(offset),
                )
        else:
            exchange(
                ("first", which), stage.at[half_of(which, 1 - mx), :],
                x_in.at[which], x_dev,
            )

    def to_second(which):
        landed(("first", which))
        if which in Z_FIRST:
            rows = pair_of(which, 0)
            summed = total[rows, :]
            for offset in range(3):
                summed = summed + z_in[which, offset].astype(F32)
        else:
            rows = half_of(which, mx)
            summed = total[rows, :] + x_in[which].astype(F32)
        total[rows, :] = summed
        stage[rows, :] = summed.astype(BF16)
        if which in Z_FIRST:
            other = rows_of(bases[which] + zi * 2 * piece + (1 - mx) * piece, piece)
            exchange(
                ("second", which), stage.at[other, :], x_in.at[which, 0:piece, :], x_dev
            )
        else:
            for offset in (2, 1, 3):
                exchange(
                    ("second", which), stage.at[piece_of(which, offset), :],
                    z_in.at[which, offset - 1, 0:piece, :], z_dev(offset),
                )

    def to_y(which):
        landed(("second", which))
        summed = total[piece_of(which, 0), :]
        if which in Z_FIRST:
            summed = summed + x_in[which, 0:piece, :].astype(F32)
        else:
            for offset in range(3):
                summed = summed + z_in[which, offset, 0:piece, :].astype(F32)
        slots[which, member] = summed.astype(BF16)
        place = slots.at[which, member]
        for offset in range(1, members):
            exchange(("y", which), place, place, m_dev(offset))

    def back_z(which):
        landed(("y", which))
        summed = slots[which, 0].astype(F32)
        for other in range(1, members):
            summed = summed + slots[which, other].astype(F32)
        full[piece_of(which, 0), mine] = (summed * scale).astype(BF16)
        for offset in (2, 1, 3):
            spread(("backz", which), piece_of(which, 0), z_dev(offset))
        spread(("backx", which), piece_of(which, 0), x_dev)

    def back_x(which):
        landed(("backz", which))
        for offset in (2, 3, 1):
            spread(("backx", which), piece_of(which, offset), x_dev)
        if which not in Z_FIRST:
            spread(("last", which), half_of(which, mx), core_dev)

    def back_core(which):
        landed(("backx", which))
        if which in Z_FIRST:
            spread(("last", which), rows_of(bases[which], span), core_dev)
        else:
            spread(("last", which), half_of(which, 1 - mx), core_dev)

    def fill_in(index):
        receive(index)
        backward(index, lambda which: None)

        @pl.when(index >= 1)
        def _():
            grad_input(index - 1)

    each(0, CHUNKS - 1, fill_in)
    receive(CHUNKS - 1)

    @pl.when(frame == 3)
    def _():
        def late(index):
            rows = pl.ds(pl.multiple_of(index * size, size), size)
            relay_last(index)
            act_t = a2[rows, :].T
            add_temporal(1, act_t, c1[rows, :])
            add_temporal(2, act_t, cot[rows, :])

        each(HALF, CHUNKS, late)

    def all_to_core(which):
        for part_of in range(SPLIT):
            to_core(which * SPLIT + part_of)

    backward(CHUNKS - 1, all_to_core)

    later = []
    actions = (to_first, to_second, to_y, back_z, back_x, back_core)
    for which in range(4 * SPLIT):
        times = Z_FIRST_AT if which in Z_FIRST else X_FIRST_AT
        for action, (when, stride) in zip(actions, times):
            later.append((when + stride * which / SPLIT, action, which))
    for index, when in GRAD_INPUT_AT:
        later.append((when, grad_input, CHUNKS - 1 - index))
    for index, when in enumerate(RELAY_AT):
        later.append((when, relay_first, index))
    for index, when in enumerate(LAST_AT):
        later.append((when, relay_last, HALF - 1 - index))
    for index, when in enumerate(HELD_AT):
        later.append((when, held, CHUNKS - HOLD + index))
    for when, start, stop in OUTPUT_AT:
        later.append((when, lambda span: each(span[0], span[1], output), (start, stop)))
    for _, action, argument in sorted(later, key=lambda entry: entry[0]):
        action(argument)
    for which in range(4 * SPLIT):
        landed(("last", which))

    @pl.when(frame == 0)
    def _():
        each(0, HALF, lambda i: left(i, rc_sem))
        each(0, VIA, lambda i: left(i, ra_sem))
        each(0, CHUNKS, lambda i: left(i, ay_sem))
        each(0, CHUNKS, lambda i: left(i, az_sem))

    @pl.when(frame == 1)
    def _():
        each(0, CHUNKS, lambda i: left(i, cy_sem))
        each(0, VIA, lambda i: left(i, ay_sem))
        each(0, CHUNKS, lambda i: left(i, az_sem))

    @pl.when(frame == 2)
    def _():
        each(0, CHUNKS, lambda i: left(i, cz_sem))
        each(HALF, CHUNKS, lambda i: left(i, cy_sem))
        each(0, CHUNKS, lambda i: left(i, ay_sem))

    @pl.when(frame == 3)
    def _():
        each(0, CHUNKS, lambda i: left(i, cy_sem))
        each(0, CHUNKS, lambda i: left(i, cz_sem))
        each(VIA, CHUNKS, lambda i: left(i, ra_sem))


def finish_kernel(
    out, gin, grads, out_hbm, gin_hbm, spatial_hbm, temporal_hbm, wide, sems
):
    block = grads.shape[0] // 4
    stores = []

    def store(source, dest):
        stores.append(pltpu.make_async_copy(source, dest, sems.at[len(stores)]))
        stores[-1].start()

    store(out, out_hbm)
    store(gin, gin_hbm)
    for index in range(4):
        part = pl.ds(index * block, block)
        wide[part, :] = grads[part, :].astype(F32)
        store(wide.at[part, :], spatial_hbm.at[part, :] if index < 3 else temporal_hbm)
    for move in stores:
        move.wait()


def local(frames_in, spatial_weight, temporal_weight, cotangent):
    slab_rows, width, channels = frames_in.shape
    sp_count = lax.axis_size("sp")
    dp_count = lax.axis_size("dp")
    members = sp_count // 4
    cells = slab_rows * width
    size = cells // CHUNKS
    lanes = channels // 2
    x = frames_in.reshape(cells, channels)
    cot = cotangent.reshape(cells, channels)
    w3 = spatial_weight.reshape(3, 3 * channels, channels)
    scale = 1.0 / math.sqrt(slab_rows * sp_count * dp_count * width)

    count = 12 * channels
    block = 3 * channels
    blocks = 4 * SPLIT
    half, piece = block // SPLIT // 2, block // SPLIT // 8
    exchanges = blocks * (14 + members - 1)
    frame = jax.ShapeDtypeStruct((cells, channels), BF16)
    slab = pltpu.VMEM((cells, channels), BF16)
    padded = pltpu.VMEM((cells + 2 * width, 3 * channels), BF16)
    vmem = pl.BlockSpec(memory_space=pltpu.VMEM)
    hbm = pl.BlockSpec(memory_space=pltpu.HBM)
    block_out, grad_in, grads = pl.pallas_call(
        functools.partial(block_kernel, width, members, scale),
        out_shape=(slab, slab, pltpu.VMEM((count, channels), BF16)),
        in_specs=[hbm] * 4,
        out_specs=(vmem,) * 3,
        scratch_shapes=[slab] * 7
        + [
            pltpu.VMEM((cells, channels), F32),
            padded,
            padded,
            pltpu.VMEM((3, block, channels), BF16),
            pltpu.VMEM((3, channels, channels), BF16),
            pltpu.VMEM((3, block, channels), BF16),
            pltpu.VMEM((3, channels, channels), BF16),
            pltpu.VMEM((size, channels), F32),
            pltpu.VMEM((count, channels), F32),
            pltpu.VMEM((count, lanes), F32),
            pltpu.VMEM((count, lanes), F32),
            pltpu.VMEM((count, lanes), BF16),
            pltpu.VMEM((blocks, half, lanes), BF16),
            pltpu.VMEM((blocks, 3, 2 * piece, lanes), BF16),
            pltpu.VMEM((blocks, members, piece, lanes), BF16),
            pltpu.SemaphoreType.DMA((4,)),
        ]
        + [pltpu.SemaphoreType.DMA((CHUNKS,))] * 10
        + [pltpu.SemaphoreType.DMA((exchanges,))] * 2,
        compiler_params=pltpu.CompilerParams(
            collective_id=0, has_side_effects=True, vmem_limit_bytes=VMEM_LIMIT
        ),
        cost_estimate=pl.CostEstimate(
            flops=72 * cells * channels * channels,
            bytes_accessed=16 * cells * channels,
            transcendentals=2 * cells * channels,
        ),
        name="video_block",
    )(x, cot, w3, temporal_weight)

    block_out, grad_in, grad_spatial, grad_temporal = pl.pallas_call(
        finish_kernel,
        out_shape=(
            frame, frame,
            jax.ShapeDtypeStruct((9 * channels, channels), F32),
            jax.ShapeDtypeStruct((3 * channels, channels), F32),
        ),
        in_specs=[vmem] * 3,
        out_specs=(hbm,) * 4,
        scratch_shapes=[pltpu.VMEM((count, channels), F32), pltpu.SemaphoreType.DMA((6,))],
        compiler_params=pltpu.CompilerParams(vmem_limit_bytes=16 * 1024 * 1024),
        name="finish",
    )(block_out, grad_in, grads)
    grad_spatial = grad_spatial.reshape(3, 3, channels, channels)
    grad_temporal = grad_temporal.reshape(3, channels, channels)
    return (
        block_out.reshape(frames_in.shape),
        grad_in.reshape(frames_in.shape),
        grad_spatial,
        grad_temporal,
    )


def solution(mesh):
    placed = (P(("dp", "sp"), None, None), P(), P(), P(("dp", "sp"), None, None))
    return jax.shard_map(
        local,
        mesh=mesh,
        in_specs=placed,
        out_specs=(P(("dp", "sp"), None, None), P(("dp", "sp"), None, None), P(), P()),
        check_vma=False,
    )
```

```python
import functools
import math

import jax
import jax.numpy as jnp
from jax import lax
from jax.experimental import pallas as pl
from jax.experimental.pallas import tpu as pltpu
from jax.sharding import PartitionSpec as P

FRAMES = 4
CHUNKS = 8
HALF = CHUNKS // 2
LEAD = CHUNKS // 8
VIA = 3
HOLD = 1
Z_FIRST = (0,)
SPLIT = 1
X_FIRST_AT = ((0.5, 0.6), (3.5, 2.1), (8.0, 2.1), (10.8, 2.1), (15.2, 2.1), (18.0, 2.1))
Z_FIRST_AT = ((0.5, 0.6), (8.0, 0.6), (11.0, 0.6), (13.8, 0.6), (18.3, 2.1), (20.9, 2.1))
HELD_AT = (19.3,)
GRAD_INPUT_AT = ((1, 3.0), (0, 3.1))
RELAY_AT = (2.5, 13.5, 21.6)
NOW = 2
LAST_AT = (5.0, 17.2, 19.6)
OWN_AT = 3.2
OLD_AT = ((9.0, 4, 6), (11.5, 6, 8), (13.6, 0, 2), (15.9, 2, 3), (19.7, 3, 4))
OUTPUT_AT = ((15.28, 4, 5), (17.38, 5, 6), (19.28, 6, 7), (21.28, 0, 1), (23.28, 7, 8), (28.1, 1, 2), (28.2, 3, 4), (28.3, 2, 3))
VMEM_LIMIT = 48 * 1024 * 1024
MESH = pl.DeviceIdType.MESH
F32 = jnp.float32
BF16 = jnp.bfloat16


def mm(left, right):
    return jnp.dot(left, right, preferred_element_type=F32)


def store_shifted(dest, offset, values, width):
    cells, channels = values.shape
    column = lax.broadcasted_iota(jnp.int32, (cells, channels), 0) % width
    before = jnp.where(column == 0, 0.0, pltpu.roll(values, 1, axis=0))
    after = jnp.where(column == width - 1, 0.0, pltpu.roll(values, cells - 1, axis=0))
    dest[pl.ds(offset, cells), 0:channels] = before.astype(BF16)
    dest[pl.ds(offset, cells), channels : 2 * channels] = values.astype(BF16)
    dest[pl.ds(offset, cells), 2 * channels : 3 * channels] = after.astype(BF16)


def zero_edges(dest, width):
    rows, lanes = dest.shape
    dest[0:width] = jnp.zeros((width, lanes), BF16)
    dest[rows - width : rows] = jnp.zeros((width, lanes), BF16)


def block_kernel(
    width, members, scale,
    x_hbm, cot_hbm, w_hbm, tw_hbm,
    out, gin, full,
    x, cot, c1, c2, a1, a2, act, slope, x3, g3, w_ref, tw_ref, wf, wt, part, acc,
    core_in, total, stage, x_in, z_in, slots,
    load_sem, c1_sem, c2_sem, a1_sem, a2_sem, cy_sem, cz_sem, ay_sem, az_sem, rc_sem, ra_sem,
    red_send, red_recv,
):
    dp = lax.axis_index("dp")
    sp = lax.axis_index("sp")
    frame = sp % FRAMES
    y = sp % 2
    zi = (sp // 2) % 4
    group = sp // 8
    member = y + 2 * group
    core = dp % 2
    mx = (dp // 2) % 2
    cells, channels = x.shape
    size = cells // CHUNKS
    lanes = channels // 2

    y_dev = (dp, sp + 1 - 2 * y)
    t_dev = (dp, sp + 2 - 4 * (zi % 2))
    core_dev = (dp + 1 - 2 * core, sp)
    x_dev = (dp + 2 - 4 * mx, sp)

    def z_member(offset):
        return (zi + offset) % 4

    def z_dev(offset):
        return (dp, sp + (z_member(offset) - zi) * 2)

    def m_dev(offset):
        other = (member + offset) % members
        return (dp, sp + other % 2 - y + (other // 2 - group) * 8)

    def chunk(ref, index):
        return ref.at[pl.ds(pl.multiple_of(index * size, size), size), :]

    def copy(source, dest, send_sem, recv_sem, device):
        return pltpu.make_async_remote_copy(
            src_ref=source, dst_ref=dest, send_sem=send_sem, recv_sem=recv_sem,
            device_id=device, device_id_type=MESH,
        )

    def send(source, dest, index, send_sems, recv_sems, device):
        copy(
            chunk(source, index), chunk(dest, index), send_sems.at[index], recv_sems.at[index], device
        ).start()

    def arrived(dest, index, recv_sems):
        copy(
            chunk(dest, index), chunk(dest, index), recv_sems.at[index], recv_sems.at[index], y_dev
        ).wait_recv()

    def left(index, send_sems):
        copy(
            chunk(act, index), chunk(act, index), send_sems.at[index], send_sems.at[index], y_dev
        ).wait_send()

    def each(start, stop, body):
        def step(index, carry):
            body(index)
            return carry

        lax.fori_loop(start, stop, step, 0)

    x_load = pltpu.make_async_copy(x_hbm, x, load_sem.at[0])
    cot_load = pltpu.make_async_copy(cot_hbm, cot, load_sem.at[1])
    w_load = pltpu.make_async_copy(w_hbm, w_ref, load_sem.at[2])
    tw_load = pltpu.make_async_copy(tw_hbm, tw_ref, load_sem.at[3])
    for load in (x_load, w_load, tw_load, cot_load):
        load.start()

    barrier = pltpu.get_barrier_semaphore()
    greeted = [core_dev, x_dev] + [z_dev(i) for i in (1, 2, 3)] + [m_dev(i) for i in range(1, members)]
    for device in greeted:
        pl.semaphore_signal(barrier, inc=1, device_id=device, device_id_type=MESH)
    pl.semaphore_wait(barrier, len(greeted))

    @pl.when(frame == 1)
    def _():
        each(0, CHUNKS, lambda i: send(cot_hbm, c1, i, cy_sem, c1_sem, y_dev))

    @pl.when(frame == 2)
    def _():
        each(0, CHUNKS, lambda i: send(cot_hbm, c2, i, cz_sem, c2_sem, t_dev))
        each(HALF, CHUNKS, lambda i: send(cot_hbm, c1, i, cy_sem, c1_sem, y_dev))

    @pl.when(frame == 3)
    def _():
        each(0, CHUNKS, lambda i: send(cot_hbm, c1, i, cy_sem, c1_sem, y_dev))
        each(0, HALF, lambda i: send(cot_hbm, c2, i, cz_sem, c2_sem, t_dev))

    acc[...] = jnp.zeros_like(acc)
    zero_edges(x3, width)
    zero_edges(g3, width)
    x_load.wait()
    w_load.wait()

    def forward(step):
        @pl.when(step < CHUNKS)
        def _():
            store_shifted(
                x3, pl.multiple_of(width + step * size, width),
                x[pl.ds(pl.multiple_of(step * size, size), size), :].astype(F32), width,
            )

        @pl.when(step >= 1)
        def _():
            index = step - 1
            base = pl.multiple_of(index * size, size)
            pre = jnp.zeros((size, channels), F32)
            for tap in range(3):
                pre = pre + mm(x3[pl.ds(base + tap * width, size), :], w_ref[tap])
            sigma = jax.nn.sigmoid(pre)
            act[pl.ds(base, size), :] = (pre * sigma).astype(BF16)
            slope[pl.ds(base, size), :] = sigma * (1.0 + pre * (1.0 - sigma))

            @pl.when(frame == 0)
            def _():
                send(act, a2, index, az_sem, a2_sem, t_dev)

            @pl.when((frame == 0) & (index < LEAD))
            def _():
                send(act, a1, index, ay_sem, a1_sem, y_dev)

            @pl.when((frame == 1) & (index < VIA))
            def _():
                send(act, a1, index, ay_sem, a1_sem, y_dev)

            @pl.when((frame == 1) & (index >= HALF))
            def _():
                send(act, a2, index, az_sem, a2_sem, t_dev)

            @pl.when((frame == 2) & (index < CHUNKS - HOLD))
            def _():
                send(act, a1, index, ay_sem, a1_sem, y_dev)

    each(0, CHUNKS + 1, forward)

    @pl.when(frame == 1)
    def _():
        each(0, HALF, lambda i: send(act, a2, HALF - 1 - i, az_sem, a2_sem, t_dev))

    tw_load.wait()
    for tap in range(3):
        wt[tap] = tw_ref[tap].T
        for side in range(3):
            wf[tap, side * channels : (side + 1) * channels, :] = w_ref[
                2 - tap, (2 - side) * channels : (3 - side) * channels, :
            ].T
    cot_load.wait()

    gt_base = 9 * channels
    block = 3 * channels

    def add_temporal(tap, act_t, other):
        acc[gt_base + tap * channels : gt_base + (tap + 1) * channels, :] += mm(act_t, other)

    def receive(index):
        rows = pl.ds(pl.multiple_of(index * size, size), size)
        early = index < HALF

        @pl.when((frame < 3) | (index >= HALF))
        def _():
            arrived(c1, index, c1_sem)

        @pl.when((frame == 0) | ((frame == 1) & early))
        def _():
            arrived(c2, index, c2_sem)

        @pl.when((frame == 0) & early)
        def _():
            send(c2, c1, index, rc_sem, c1_sem, y_dev)

        @pl.when((frame == 0) & (index == HALF - 1))
        def _():
            each(LEAD, CHUNKS - HOLD, lambda i: send(act, a1, i, ay_sem, a1_sem, y_dev))

        @pl.when((frame == 3) & (index >= HALF))
        def _():
            c2[rows, :] = (mm(c1[rows, :], wt[1]) + mm(cot[rows, :], wt[2])).astype(BF16)
            send(c2, c1, index, cz_sem, c1_sem, t_dev)

    def backward(index, finish):
        base = pl.multiple_of(index * size, size)
        rows = pl.ds(base, size)
        early = index < HALF
        act_t = act[rows, :].T
        part[...] = mm(cot[rows, :], wt[0])
        add_temporal(0, act_t, cot[rows, :])

        @pl.when((frame == 0) | (frame == 2) | ((frame == 1) & early))
        def _():
            part[...] += mm(c1[rows, :], wt[1])
            add_temporal(1, act_t, c1[rows, :])

        @pl.when((frame == 0) | ((frame == 1) & early))
        def _():
            part[...] += mm(c2[rows, :], wt[2])
            add_temporal(2, act_t, c2[rows, :])

        finish(0)

        @pl.when((frame == 1) & (index >= HALF))
        def _():
            part[...] += c1[rows, :].astype(F32)

        grad_pre = part[...].astype(BF16).astype(F32) * slope[rows, :]
        store_shifted(g3, pl.multiple_of(width + base, width), grad_pre, width)
        grad_pre = grad_pre.astype(BF16)
        for tap in range(3):
            window = x3[pl.ds(base + tap * width, size), :]
            acc[tap * block : (tap + 1) * block, :] += mm(window.T, grad_pre)
            finish(1 + tap)

    def grad_input(index):
        base = pl.multiple_of(index * size, size)
        total_in = cot[pl.ds(base, size), :].astype(F32)
        for tap in range(3):
            total_in = total_in + mm(g3[pl.ds(base + tap * width, size), :], wf[tap])
        gin[pl.ds(base, size), :] = total_in.astype(BF16)

    def own_term(index):
        rows = pl.ds(pl.multiple_of(index * size, size), size)
        slope[rows, :] = mm(act[rows, :], tw_ref[0])

    def old_term(index):
        rows = pl.ds(pl.multiple_of(index * size, size), size)

        @pl.when((frame == 2) | ((frame == 3) & (index < VIA)))
        def _():
            arrived(a2, index, a2_sem)

        @pl.when(frame >= 2)
        def _():
            slope[rows, :] += mm(a2[rows, :], tw_ref[2])

    def output(index):
        rows = pl.ds(pl.multiple_of(index * size, size), size)

        def write(temporal):
            temporal = temporal.astype(BF16).astype(F32)
            out[rows, :] = (x[rows, :].astype(F32) + temporal).astype(BF16)

        @pl.when(frame == 0)
        def _():
            write(slope[rows, :])

        @pl.when(frame >= 1)
        def _():
            arrived(a1, index, a1_sem)
            write(slope[rows, :] + mm(a1[rows, :], tw_ref[1]))

    def relay_first(index):
        @pl.when(frame == 0)
        def _():
            arrived(a1, index, a1_sem)
            send(a1, a1, index, ra_sem, a1_sem, t_dev)

    def relay_last(index):
        @pl.when(frame == 3)
        def _():
            if index < HALF:
                arrived(a2, index, a2_sem)
            send(a2, a1, index, ra_sem, a1_sem, y_dev)

    def held(index):
        @pl.when((frame == 0) | (frame == 2))
        def _():
            send(act, a1, index, ay_sem, a1_sem, y_dev)

    span = block // SPLIT
    half, piece = span // 2, span // 8
    keep = pl.multiple_of(core * lanes, lanes)
    give = pl.multiple_of((1 - core) * lanes, lanes)
    mine = pl.ds(keep, lanes)
    bases = [
        start + part_of * span
        for start in [gt_base] + [tap * block for tap in range(3)]
        for part_of in range(SPLIT)
    ]
    used = []
    moving = {}

    def exchange(name, source, dest, device):
        slot = len(used)
        used.append(slot)
        moved = copy(source, dest, red_send.at[slot], red_recv.at[slot], device)
        moved.start()
        moving.setdefault(name, []).append(moved)

    def landed(name):
        for moved in moving.pop(name):
            moved.wait()

    def rows_of(start, length):
        return pl.ds(pl.multiple_of(start, 16), length)

    def half_of(which, part_x):
        return rows_of(bases[which] + part_x * half, half)

    def piece_of(which, offset):
        if which in Z_FIRST:
            return rows_of(bases[which] + z_member(offset) * 2 * piece + mx * piece, piece)
        return rows_of(bases[which] + mx * half + z_member(offset) * piece, piece)

    def pair_of(which, offset):
        return rows_of(bases[which] + z_member(offset) * 2 * piece, 2 * piece)

    def spread(name, rows, device):
        place = full.at[rows, mine]
        exchange(name, place, place, device)

    def to_core(which):
        rows = rows_of(bases[which], span)
        exchange(("core", which), acc.at[rows, pl.ds(give, lanes)], core_in.at[rows, :], core_dev)

    def to_first(which):
        landed(("core", which))
        rows = rows_of(bases[which], span)
        summed = acc[rows, mine] + core_in[rows, :]
        total[rows, :] = summed
        stage[rows, :] = summed.astype(BF16)
        if which in Z_FIRST:
            for offset in (2, 1, 3):
                exchange(
                    ("first", which), stage.at[pair_of(which, offset), :],
                    z_in.at[which, offset - 1], z_dev(offset),
                )
        else:
            exchange(
                ("first", which), stage.at[half_of(which, 1 - mx), :],
                x_in.at[which], x_dev,
            )

    def to_second(which):
        landed(("first", which))
        if which in Z_FIRST:
            rows = pair_of(which, 0)
            summed = total[rows, :]
            for offset in range(3):
                summed = summed + z_in[which, offset].astype(F32)
        else:
            rows = half_of(which, mx)
            summed = total[rows, :] + x_in[which].astype(F32)
        total[rows, :] = summed
        stage[rows, :] = summed.astype(BF16)
        if which in Z_FIRST:
            other = rows_of(bases[which] + zi * 2 * piece + (1 - mx) * piece, piece)
            exchange(
                ("second", which), stage.at[other, :], x_in.at[which, 0:piece, :], x_dev
            )
        else:
            for offset in (2, 1, 3):
                exchange(
                    ("second", which), stage.at[piece_of(which, offset), :],
                    z_in.at[which, offset - 1, 0:piece, :], z_dev(offset),
                )

    def to_y(which):
        landed(("second", which))
        summed = total[piece_of(which, 0), :]
        if which in Z_FIRST:
            summed = summed + x_in[which, 0:piece, :].astype(F32)
        else:
            for offset in range(3):
                summed = summed + z_in[which, offset, 0:piece, :].astype(F32)
        slots[which, member] = summed.astype(BF16)
        place = slots.at[which, member]
        for offset in range(1, members):
            exchange(("y", which), place, place, m_dev(offset))

    def back_z(which):
        landed(("y", which))
        summed = slots[which, 0].astype(F32)
        for other in range(1, members):
            summed = summed + slots[which, other].astype(F32)
        full[piece_of(which, 0), mine] = (summed * scale).astype(BF16)
        for offset in (2, 1, 3):
            spread(("backz", which), piece_of(which, 0), z_dev(offset))
        spread(("backx", which), piece_of(which, 0), x_dev)

    def back_x(which):
        landed(("backz", which))
        for offset in (2, 3, 1):
            spread(("backx", which), piece_of(which, offset), x_dev)
        if which not in Z_FIRST:
            spread(("last", which), half_of(which, mx), core_dev)

    def back_core(which):
        landed(("backx", which))
        if which in Z_FIRST:
            spread(("last", which), rows_of(bases[which], span), core_dev)
        else:
            spread(("last", which), half_of(which, 1 - mx), core_dev)

    def fill_in(index):
        receive(index)
        backward(index, lambda which: None)

        @pl.when(index >= 1)
        def _():
            grad_input(index - 1)

        own_term(index)

    each(0, CHUNKS - 1, fill_in)
    receive(CHUNKS - 1)

    @pl.when(frame == 3)
    def _():
        def late(index):
            rows = pl.ds(pl.multiple_of(index * size, size), size)
            arrived(a2, index, a2_sem)

            @pl.when(index < HALF + NOW)
            def _():
                send(a2, a1, index, ra_sem, a1_sem, y_dev)

            act_t = a2[rows, :].T
            add_temporal(1, act_t, c1[rows, :])
            add_temporal(2, act_t, cot[rows, :])

        each(HALF, CHUNKS, late)

    def all_to_core(which):
        for part_of in range(SPLIT):
            to_core(which * SPLIT + part_of)

    backward(CHUNKS - 1, all_to_core)

    later = []
    actions = (to_first, to_second, to_y, back_z, back_x, back_core)
    for which in range(4 * SPLIT):
        times = Z_FIRST_AT if which in Z_FIRST else X_FIRST_AT
        for action, (when, stride) in zip(actions, times):
            later.append((when + stride * which / SPLIT, action, which))
    for index, when in GRAD_INPUT_AT:
        later.append((when, grad_input, CHUNKS - 1 - index))
    later.append((OWN_AT, own_term, CHUNKS - 1))
    for when, start, stop in OLD_AT:
        later.append((when, lambda span: each(span[0], span[1], old_term), (start, stop)))
    for index, when in enumerate(RELAY_AT):
        later.append((when, relay_first, index))
    waiting = [*range(HALF + NOW, CHUNKS), *range(HALF - 1, VIA - 1, -1)]
    for index, when in zip(waiting, LAST_AT):
        later.append((when, relay_last, index))
    for index, when in enumerate(HELD_AT):
        later.append((when, held, CHUNKS - HOLD + index))
    for when, start, stop in OUTPUT_AT:
        later.append((when, lambda span: each(span[0], span[1], output), (start, stop)))
    for _, action, argument in sorted(later, key=lambda entry: entry[0]):
        action(argument)
    for which in range(4 * SPLIT):
        landed(("last", which))

    @pl.when(frame == 0)
    def _():
        each(0, HALF, lambda i: left(i, rc_sem))
        each(0, VIA, lambda i: left(i, ra_sem))
        each(0, CHUNKS, lambda i: left(i, ay_sem))
        each(0, CHUNKS, lambda i: left(i, az_sem))

    @pl.when(frame == 1)
    def _():
        each(0, CHUNKS, lambda i: left(i, cy_sem))
        each(0, VIA, lambda i: left(i, ay_sem))
        each(0, CHUNKS, lambda i: left(i, az_sem))

    @pl.when(frame == 2)
    def _():
        each(0, CHUNKS, lambda i: left(i, cz_sem))
        each(HALF, CHUNKS, lambda i: left(i, cy_sem))
        each(0, CHUNKS, lambda i: left(i, ay_sem))

    @pl.when(frame == 3)
    def _():
        each(0, CHUNKS, lambda i: left(i, cy_sem))
        each(0, CHUNKS, lambda i: left(i, cz_sem))
        each(VIA, CHUNKS, lambda i: left(i, ra_sem))


def finish_kernel(
    out, gin, grads, out_hbm, gin_hbm, spatial_hbm, temporal_hbm, wide, sems
):
    block = grads.shape[0] // 4
    stores = []

    def store(source, dest):
        stores.append(pltpu.make_async_copy(source, dest, sems.at[len(stores)]))
        stores[-1].start()

    store(out, out_hbm)
    store(gin, gin_hbm)
    for index in range(4):
        part = pl.ds(index * block, block)
        wide[part, :] = grads[part, :].astype(F32)
        store(wide.at[part, :], spatial_hbm.at[part, :] if index < 3 else temporal_hbm)
    for move in stores:
        move.wait()


def local(frames_in, spatial_weight, temporal_weight, cotangent):
    slab_rows, width, channels = frames_in.shape
    sp_count = lax.axis_size("sp")
    dp_count = lax.axis_size("dp")
    members = sp_count // 4
    cells = slab_rows * width
    size = cells // CHUNKS
    lanes = channels // 2
    x = frames_in.reshape(cells, channels)
    cot = cotangent.reshape(cells, channels)
    w3 = spatial_weight.reshape(3, 3 * channels, channels)
    scale = 1.0 / math.sqrt(slab_rows * sp_count * dp_count * width)

    count = 12 * channels
    block = 3 * channels
    blocks = 4 * SPLIT
    half, piece = block // SPLIT // 2, block // SPLIT // 8
    exchanges = blocks * (14 + members - 1)
    frame = jax.ShapeDtypeStruct((cells, channels), BF16)
    slab = pltpu.VMEM((cells, channels), BF16)
    padded = pltpu.VMEM((cells + 2 * width, 3 * channels), BF16)
    vmem = pl.BlockSpec(memory_space=pltpu.VMEM)
    hbm = pl.BlockSpec(memory_space=pltpu.HBM)
    block_out, grad_in, grads = pl.pallas_call(
        functools.partial(block_kernel, width, members, scale),
        out_shape=(slab, slab, pltpu.VMEM((count, channels), BF16)),
        in_specs=[hbm] * 4,
        out_specs=(vmem,) * 3,
        scratch_shapes=[slab] * 7
        + [
            pltpu.VMEM((cells, channels), F32),
            padded,
            padded,
            pltpu.VMEM((3, block, channels), BF16),
            pltpu.VMEM((3, channels, channels), BF16),
            pltpu.VMEM((3, block, channels), BF16),
            pltpu.VMEM((3, channels, channels), BF16),
            pltpu.VMEM((size, channels), F32),
            pltpu.VMEM((count, channels), F32),
            pltpu.VMEM((count, lanes), F32),
            pltpu.VMEM((count, lanes), F32),
            pltpu.VMEM((count, lanes), BF16),
            pltpu.VMEM((blocks, half, lanes), BF16),
            pltpu.VMEM((blocks, 3, 2 * piece, lanes), BF16),
            pltpu.VMEM((blocks, members, piece, lanes), BF16),
            pltpu.SemaphoreType.DMA((4,)),
        ]
        + [pltpu.SemaphoreType.DMA((CHUNKS,))] * 10
        + [pltpu.SemaphoreType.DMA((exchanges,))] * 2,
        compiler_params=pltpu.CompilerParams(
            collective_id=0, has_side_effects=True, vmem_limit_bytes=VMEM_LIMIT
        ),
        cost_estimate=pl.CostEstimate(
            flops=72 * cells * channels * channels,
            bytes_accessed=16 * cells * channels,
            transcendentals=2 * cells * channels,
        ),
        name="video_block",
    )(x, cot, w3, temporal_weight)

    block_out, grad_in, grad_spatial, grad_temporal = pl.pallas_call(
        finish_kernel,
        out_shape=(
            frame, frame,
            jax.ShapeDtypeStruct((9 * channels, channels), F32),
            jax.ShapeDtypeStruct((3 * channels, channels), F32),
        ),
        in_specs=[vmem] * 3,
        out_specs=(hbm,) * 4,
        scratch_shapes=[pltpu.VMEM((count, channels), F32), pltpu.SemaphoreType.DMA((6,))],
        compiler_params=pltpu.CompilerParams(vmem_limit_bytes=16 * 1024 * 1024),
        name="finish",
    )(block_out, grad_in, grads)
    grad_spatial = grad_spatial.reshape(3, 3, channels, channels)
    grad_temporal = grad_temporal.reshape(3, channels, channels)
    return (
        block_out.reshape(frames_in.shape),
        grad_in.reshape(frames_in.shape),
        grad_spatial,
        grad_temporal,
    )


def solution(mesh):
    placed = (P(("dp", "sp"), None, None), P(), P(), P(("dp", "sp"), None, None))
    return jax.shard_map(
        local,
        mesh=mesh,
        in_specs=placed,
        out_specs=(P(("dp", "sp"), None, None), P(("dp", "sp"), None, None), P(), P()),
        check_vma=False,
    )
```

```python
import functools
import math

import jax
import jax.numpy as jnp
from jax import lax
from jax.experimental import pallas as pl
from jax.experimental.pallas import tpu as pltpu
from jax.sharding import PartitionSpec as P

FRAMES = 4
CHUNKS = 8
HALF = CHUNKS // 2
LEAD = CHUNKS // 8
VIA = 3
HOLD = 1
Z_FIRST = (0,)
SPLIT = 1
X_FIRST_AT = ((0.5, 0.6), (3.5, 2.1), (8.0, 2.1), (10.8, 2.1), (15.2, 2.1), (18.0, 2.1))
Z_FIRST_AT = ((0.5, 0.6), (8.0, 0.6), (11.0, 0.6), (13.8, 0.6), (18.3, 2.1), (20.9, 2.1))
HELD_AT = (19.3,)
GRAD_INPUT_AT = ((1, 3.0), (0, 3.1))
RELAY_AT = (2.5, 13.5, 21.6)
NOW = 2
LAST_AT = (5.0, 17.2, 19.6)
OWN_AT = 3.2
OLD_AT = ((9.0, 4, 6), (11.5, 6, 8), (13.6, 0, 2), (15.9, 2, 3), (19.7, 3, 4))
OUTPUT_AT = ((15.28, 4, 5), (17.38, 5, 6), (19.28, 6, 7), (21.28, 0, 1), (23.28, 7, 8), (28.1, 1, 2), (28.2, 3, 4), (28.3, 2, 3))
VMEM_LIMIT = 50 * 1024 * 1024
MESH = pl.DeviceIdType.MESH
F32 = jnp.float32
BF16 = jnp.bfloat16


def mm(left, right):
    return jnp.dot(left, right, preferred_element_type=F32)


def store_shifted(dest, offset, values, width):
    cells, channels = values.shape
    column = lax.broadcasted_iota(jnp.int32, (cells, channels), 0) % width
    before = jnp.where(column == 0, 0.0, pltpu.roll(values, 1, axis=0))
    after = jnp.where(column == width - 1, 0.0, pltpu.roll(values, cells - 1, axis=0))
    dest[pl.ds(offset, cells), 0:channels] = before.astype(BF16)
    dest[pl.ds(offset, cells), channels : 2 * channels] = values.astype(BF16)
    dest[pl.ds(offset, cells), 2 * channels : 3 * channels] = after.astype(BF16)


def zero_edges(dest, width):
    rows, lanes = dest.shape
    dest[0:width] = jnp.zeros((width, lanes), BF16)
    dest[rows - width : rows] = jnp.zeros((width, lanes), BF16)


def block_kernel(
    width, members, scale,
    x_hbm, cot_hbm, w_hbm, tw_hbm,
    out, gin, full,
    x, cot, c1, c2, a1, a2, act, slope, x3, g3, w_ref, tw_ref, wf, wt, part, act_last, x_last, acc,
    core_in, total, stage, x_in, z_in, slots,
    load_sem, c1_sem, c2_sem, a1_sem, a2_sem, cy_sem, cz_sem, ay_sem, az_sem, rc_sem, ra_sem,
    red_send, red_recv,
):
    dp = lax.axis_index("dp")
    sp = lax.axis_index("sp")
    frame = sp % FRAMES
    y = sp % 2
    zi = (sp // 2) % 4
    group = sp // 8
    member = y + 2 * group
    core = dp % 2
    mx = (dp // 2) % 2
    cells, channels = x.shape
    size = cells // CHUNKS
    lanes = channels // 2

    y_dev = (dp, sp + 1 - 2 * y)
    t_dev = (dp, sp + 2 - 4 * (zi % 2))
    core_dev = (dp + 1 - 2 * core, sp)
    x_dev = (dp + 2 - 4 * mx, sp)

    def z_member(offset):
        return (zi + offset) % 4

    def z_dev(offset):
        return (dp, sp + (z_member(offset) - zi) * 2)

    def m_dev(offset):
        other = (member + offset) % members
        return (dp, sp + other % 2 - y + (other // 2 - group) * 8)

    def chunk(ref, index):
        return ref.at[pl.ds(pl.multiple_of(index * size, size), size), :]

    def copy(source, dest, send_sem, recv_sem, device):
        return pltpu.make_async_remote_copy(
            src_ref=source, dst_ref=dest, send_sem=send_sem, recv_sem=recv_sem,
            device_id=device, device_id_type=MESH,
        )

    def send(source, dest, index, send_sems, recv_sems, device):
        copy(
            chunk(source, index), chunk(dest, index), send_sems.at[index], recv_sems.at[index], device
        ).start()

    def arrived(dest, index, recv_sems):
        copy(
            chunk(dest, index), chunk(dest, index), recv_sems.at[index], recv_sems.at[index], y_dev
        ).wait_recv()

    def left(index, send_sems):
        copy(
            chunk(act, index), chunk(act, index), send_sems.at[index], send_sems.at[index], y_dev
        ).wait_send()

    def each(start, stop, body):
        def step(index, carry):
            body(index)
            return carry

        lax.fori_loop(start, stop, step, 0)

    x_load = pltpu.make_async_copy(x_hbm, x, load_sem.at[0])
    cot_load = pltpu.make_async_copy(cot_hbm, cot, load_sem.at[1])
    w_load = pltpu.make_async_copy(w_hbm, w_ref, load_sem.at[2])
    tw_load = pltpu.make_async_copy(tw_hbm, tw_ref, load_sem.at[3])
    for load in (x_load, w_load, tw_load, cot_load):
        load.start()

    barrier = pltpu.get_barrier_semaphore()
    greeted = [core_dev, x_dev] + [z_dev(i) for i in (1, 2, 3)] + [m_dev(i) for i in range(1, members)]
    for device in greeted:
        pl.semaphore_signal(barrier, inc=1, device_id=device, device_id_type=MESH)
    pl.semaphore_wait(barrier, len(greeted))

    @pl.when(frame == 1)
    def _():
        each(0, CHUNKS, lambda i: send(cot_hbm, c1, i, cy_sem, c1_sem, y_dev))

    @pl.when(frame == 2)
    def _():
        each(0, CHUNKS, lambda i: send(cot_hbm, c2, i, cz_sem, c2_sem, t_dev))
        each(HALF, CHUNKS, lambda i: send(cot_hbm, c1, i, cy_sem, c1_sem, y_dev))

    @pl.when(frame == 3)
    def _():
        each(0, CHUNKS, lambda i: send(cot_hbm, c1, i, cy_sem, c1_sem, y_dev))
        each(0, HALF, lambda i: send(cot_hbm, c2, i, cz_sem, c2_sem, t_dev))

    acc[...] = jnp.zeros_like(acc)
    zero_edges(x3, width)
    zero_edges(g3, width)
    x_load.wait()
    w_load.wait()

    def forward(step):
        @pl.when(step < CHUNKS)
        def _():
            store_shifted(
                x3, pl.multiple_of(width + step * size, width),
                x[pl.ds(pl.multiple_of(step * size, size), size), :].astype(F32), width,
            )

        @pl.when(step >= 1)
        def _():
            index = step - 1
            base = pl.multiple_of(index * size, size)
            pre = jnp.zeros((size, channels), F32)
            for tap in range(3):
                pre = pre + mm(x3[pl.ds(base + tap * width, size), :], w_ref[tap])
            sigma = jax.nn.sigmoid(pre)
            act[pl.ds(base, size), :] = (pre * sigma).astype(BF16)
            slope[pl.ds(base, size), :] = sigma * (1.0 + pre * (1.0 - sigma))

            @pl.when(frame == 0)
            def _():
                send(act, a2, index, az_sem, a2_sem, t_dev)

            @pl.when((frame == 0) & (index < LEAD))
            def _():
                send(act, a1, index, ay_sem, a1_sem, y_dev)

            @pl.when((frame == 1) & (index < VIA))
            def _():
                send(act, a1, index, ay_sem, a1_sem, y_dev)

            @pl.when((frame == 1) & (index >= HALF))
            def _():
                send(act, a2, index, az_sem, a2_sem, t_dev)

            @pl.when((frame == 2) & (index < CHUNKS - HOLD))
            def _():
                send(act, a1, index, ay_sem, a1_sem, y_dev)

    each(0, CHUNKS + 1, forward)

    @pl.when(frame == 1)
    def _():
        each(0, HALF, lambda i: send(act, a2, HALF - 1 - i, az_sem, a2_sem, t_dev))

    tw_load.wait()
    for tap in range(3):
        wt[tap] = tw_ref[tap].T
        for side in range(3):
            wf[tap, side * channels : (side + 1) * channels, :] = w_ref[
                2 - tap, (2 - side) * channels : (3 - side) * channels, :
            ].T
    cot_load.wait()

    gt_base = 9 * channels
    block = 3 * channels

    def add_temporal(tap, act_t, other):
        acc[gt_base + tap * channels : gt_base + (tap + 1) * channels, :] += mm(act_t, other)

    def receive(index):
        rows = pl.ds(pl.multiple_of(index * size, size), size)
        early = index < HALF

        @pl.when((frame < 3) | (index >= HALF))
        def _():
            arrived(c1, index, c1_sem)

        @pl.when((frame == 0) | ((frame == 1) & early))
        def _():
            arrived(c2, index, c2_sem)

        @pl.when((frame == 0) & early)
        def _():
            send(c2, c1, index, rc_sem, c1_sem, y_dev)

        @pl.when((frame == 0) & (index == HALF - 1))
        def _():
            each(LEAD, CHUNKS - HOLD, lambda i: send(act, a1, i, ay_sem, a1_sem, y_dev))

        @pl.when((frame == 3) & (index >= HALF))
        def _():
            c2[rows, :] = (mm(c1[rows, :], wt[1]) + mm(cot[rows, :], wt[2])).astype(BF16)
            send(c2, c1, index, cz_sem, c1_sem, t_dev)

    def own_gradient(index):
        rows = pl.ds(pl.multiple_of(index * size, size), size)
        act_t = act[rows, :].T
        part[...] = mm(cot[rows, :], wt[0])
        add_temporal(0, act_t, cot[rows, :])
        return act_t

    def backward(index, finish, last=False):
        base = pl.multiple_of(index * size, size)
        rows = pl.ds(base, size)
        early = index < HALF
        act_t = act_last[...] if last else own_gradient(index)

        @pl.when((frame == 0) | (frame == 2) | ((frame == 1) & early))
        def _():
            part[...] += mm(c1[rows, :], wt[1])
            add_temporal(1, act_t, c1[rows, :])

        @pl.when((frame == 0) | ((frame == 1) & early))
        def _():
            part[...] += mm(c2[rows, :], wt[2])
            add_temporal(2, act_t, c2[rows, :])

        finish(0)

        @pl.when((frame == 1) & (index >= HALF))
        def _():
            part[...] += c1[rows, :].astype(F32)

        grad_pre = part[...].astype(BF16).astype(F32) * slope[rows, :]
        store_shifted(g3, pl.multiple_of(width + base, width), grad_pre, width)
        grad_pre = grad_pre.astype(BF16)
        for tap in range(3):
            window_t = x_last[tap] if last else x3[pl.ds(base + tap * width, size), :].T
            acc[tap * block : (tap + 1) * block, :] += mm(window_t, grad_pre)
            finish(1 + tap)

    def grad_input(index):
        base = pl.multiple_of(index * size, size)
        total_in = cot[pl.ds(base, size), :].astype(F32)
        for tap in range(3):
            total_in = total_in + mm(g3[pl.ds(base + tap * width, size), :], wf[tap])
        gin[pl.ds(base, size), :] = total_in.astype(BF16)

    def own_term(index):
        rows = pl.ds(pl.multiple_of(index * size, size), size)
        slope[rows, :] = mm(act[rows, :], tw_ref[0])

    def old_term(index):
        rows = pl.ds(pl.multiple_of(index * size, size), size)

        @pl.when((frame == 2) | ((frame == 3) & (index < VIA)))
        def _():
            arrived(a2, index, a2_sem)

        @pl.when(frame >= 2)
        def _():
            slope[rows, :] += mm(a2[rows, :], tw_ref[2])

    def output(index):
        rows = pl.ds(pl.multiple_of(index * size, size), size)

        def write(temporal):
            temporal = temporal.astype(BF16).astype(F32)
            out[rows, :] = (x[rows, :].astype(F32) + temporal).astype(BF16)

        @pl.when(frame == 0)
        def _():
            write(slope[rows, :])

        @pl.when(frame >= 1)
        def _():
            arrived(a1, index, a1_sem)
            write(slope[rows, :] + mm(a1[rows, :], tw_ref[1]))

    def relay_first(index):
        @pl.when(frame == 0)
        def _():
            arrived(a1, index, a1_sem)
            send(a1, a1, index, ra_sem, a1_sem, t_dev)

    def relay_last(index):
        @pl.when(frame == 3)
        def _():
            if index < HALF:
                arrived(a2, index, a2_sem)
            send(a2, a1, index, ra_sem, a1_sem, y_dev)

    def held(index):
        @pl.when((frame == 0) | (frame == 2))
        def _():
            send(act, a1, index, ay_sem, a1_sem, y_dev)

    span = block // SPLIT
    half, piece = span // 2, span // 8
    keep = pl.multiple_of(core * lanes, lanes)
    give = pl.multiple_of((1 - core) * lanes, lanes)
    mine = pl.ds(keep, lanes)
    bases = [
        start + part_of * span
        for start in [gt_base] + [tap * block for tap in range(3)]
        for part_of in range(SPLIT)
    ]
    used = []
    moving = {}

    def exchange(name, source, dest, device):
        slot = len(used)
        used.append(slot)
        moved = copy(source, dest, red_send.at[slot], red_recv.at[slot], device)
        moved.start()
        moving.setdefault(name, []).append(moved)

    def landed(name):
        for moved in moving.pop(name):
            moved.wait()

    def rows_of(start, length):
        return pl.ds(pl.multiple_of(start, 16), length)

    def half_of(which, part_x):
        return rows_of(bases[which] + part_x * half, half)

    def piece_of(which, offset):
        if which in Z_FIRST:
            return rows_of(bases[which] + z_member(offset) * 2 * piece + mx * piece, piece)
        return rows_of(bases[which] + mx * half + z_member(offset) * piece, piece)

    def pair_of(which, offset):
        return rows_of(bases[which] + z_member(offset) * 2 * piece, 2 * piece)

    def spread(name, rows, device):
        place = full.at[rows, mine]
        exchange(name, place, place, device)

    def to_core(which):
        rows = rows_of(bases[which], span)
        exchange(("core", which), acc.at[rows, pl.ds(give, lanes)], core_in.at[rows, :], core_dev)

    def to_first(which):
        landed(("core", which))
        rows = rows_of(bases[which], span)
        summed = acc[rows, mine] + core_in[rows, :]
        total[rows, :] = summed
        stage[rows, :] = summed.astype(BF16)
        if which in Z_FIRST:
            for offset in (2, 1, 3):
                exchange(
                    ("first", which), stage.at[pair_of(which, offset), :],
                    z_in.at[which, offset - 1], z_dev(offset),
                )
        else:
            exchange(
                ("first", which), stage.at[half_of(which, 1 - mx), :],
                x_in.at[which], x_dev,
            )

    def to_second(which):
        landed(("first", which))
        if which in Z_FIRST:
            rows = pair_of(which, 0)
            summed = total[rows, :]
            for offset in range(3):
                summed = summed + z_in[which, offset].astype(F32)
        else:
            rows = half_of(which, mx)
            summed = total[rows, :] + x_in[which].astype(F32)
        total[rows, :] = summed
        stage[rows, :] = summed.astype(BF16)
        if which in Z_FIRST:
            other = rows_of(bases[which] + zi * 2 * piece + (1 - mx) * piece, piece)
            exchange(
                ("second", which), stage.at[other, :], x_in.at[which, 0:piece, :], x_dev
            )
        else:
            for offset in (2, 1, 3):
                exchange(
                    ("second", which), stage.at[piece_of(which, offset), :],
                    z_in.at[which, offset - 1, 0:piece, :], z_dev(offset),
                )

    def to_y(which):
        landed(("second", which))
        summed = total[piece_of(which, 0), :]
        if which in Z_FIRST:
            summed = summed + x_in[which, 0:piece, :].astype(F32)
        else:
            for offset in range(3):
                summed = summed + z_in[which, offset, 0:piece, :].astype(F32)
        slots[which, member] = summed.astype(BF16)
        place = slots.at[which, member]
        for offset in range(1, members):
            exchange(("y", which), place, place, m_dev(offset))

    def back_z(which):
        landed(("y", which))
        summed = slots[which, 0].astype(F32)
        for other in range(1, members):
            summed = summed + slots[which, other].astype(F32)
        full[piece_of(which, 0), mine] = (summed * scale).astype(BF16)
        for offset in (2, 1, 3):
            spread(("backz", which), piece_of(which, 0), z_dev(offset))
        spread(("backx", which), piece_of(which, 0), x_dev)

    def back_x(which):
        landed(("backz", which))
        for offset in (2, 3, 1):
            spread(("backx", which), piece_of(which, offset), x_dev)
        if which not in Z_FIRST:
            spread(("last", which), half_of(which, mx), core_dev)

    def back_core(which):
        landed(("backx", which))
        if which in Z_FIRST:
            spread(("last", which), rows_of(bases[which], span), core_dev)
        else:
            spread(("last", which), half_of(which, 1 - mx), core_dev)

    def fill_in(index):
        receive(index)
        backward(index, lambda which: None)

        @pl.when(index >= 1)
        def _():
            grad_input(index - 1)

        own_term(index)

    each(0, CHUNKS - 1, fill_in)
    act_last[...] = own_gradient(CHUNKS - 1)
    for tap in range(3):
        start = (CHUNKS - 1) * size + tap * width
        x_last[tap] = x3[start : start + size, :].T
    receive(CHUNKS - 1)

    @pl.when(frame == 3)
    def _():
        def late(index):
            rows = pl.ds(pl.multiple_of(index * size, size), size)
            arrived(a2, index, a2_sem)

            @pl.when(index < HALF + NOW)
            def _():
                send(a2, a1, index, ra_sem, a1_sem, y_dev)

            act_t = a2[rows, :].T
            add_temporal(1, act_t, c1[rows, :])
            add_temporal(2, act_t, cot[rows, :])

        each(HALF, CHUNKS, late)

    def all_to_core(which):
        for part_of in range(SPLIT):
            to_core(which * SPLIT + part_of)

    backward(CHUNKS - 1, all_to_core, last=True)

    later = []
    actions = (to_first, to_second, to_y, back_z, back_x, back_core)
    for which in range(4 * SPLIT):
        times = Z_FIRST_AT if which in Z_FIRST else X_FIRST_AT
        for action, (when, stride) in zip(actions, times):
            later.append((when + stride * which / SPLIT, action, which))
    for index, when in GRAD_INPUT_AT:
        later.append((when, grad_input, CHUNKS - 1 - index))
    later.append((OWN_AT, own_term, CHUNKS - 1))
    for when, start, stop in OLD_AT:
        later.append((when, lambda span: each(span[0], span[1], old_term), (start, stop)))
    for index, when in enumerate(RELAY_AT):
        later.append((when, relay_first, index))
    waiting = [*range(HALF + NOW, CHUNKS), *range(HALF - 1, VIA - 1, -1)]
    for index, when in zip(waiting, LAST_AT):
        later.append((when, relay_last, index))
    for index, when in enumerate(HELD_AT):
        later.append((when, held, CHUNKS - HOLD + index))
    for when, start, stop in OUTPUT_AT:
        later.append((when, lambda span: each(span[0], span[1], output), (start, stop)))
    for _, action, argument in sorted(later, key=lambda entry: entry[0]):
        action(argument)
    for which in range(4 * SPLIT):
        landed(("last", which))

    @pl.when(frame == 0)
    def _():
        each(0, HALF, lambda i: left(i, rc_sem))
        each(0, VIA, lambda i: left(i, ra_sem))
        each(0, CHUNKS, lambda i: left(i, ay_sem))
        each(0, CHUNKS, lambda i: left(i, az_sem))

    @pl.when(frame == 1)
    def _():
        each(0, CHUNKS, lambda i: left(i, cy_sem))
        each(0, VIA, lambda i: left(i, ay_sem))
        each(0, CHUNKS, lambda i: left(i, az_sem))

    @pl.when(frame == 2)
    def _():
        each(0, CHUNKS, lambda i: left(i, cz_sem))
        each(HALF, CHUNKS, lambda i: left(i, cy_sem))
        each(0, CHUNKS, lambda i: left(i, ay_sem))

    @pl.when(frame == 3)
    def _():
        each(0, CHUNKS, lambda i: left(i, cy_sem))
        each(0, CHUNKS, lambda i: left(i, cz_sem))
        each(VIA, CHUNKS, lambda i: left(i, ra_sem))


def finish_kernel(
    out, gin, grads, out_hbm, gin_hbm, spatial_hbm, temporal_hbm, wide, sems
):
    block = grads.shape[0] // 4
    stores = []

    def store(source, dest):
        stores.append(pltpu.make_async_copy(source, dest, sems.at[len(stores)]))
        stores[-1].start()

    store(out, out_hbm)
    store(gin, gin_hbm)
    for index in range(4):
        part = pl.ds(index * block, block)
        wide[part, :] = grads[part, :].astype(F32)
        store(wide.at[part, :], spatial_hbm.at[part, :] if index < 3 else temporal_hbm)
    for move in stores:
        move.wait()


def local(frames_in, spatial_weight, temporal_weight, cotangent):
    slab_rows, width, channels = frames_in.shape
    sp_count = lax.axis_size("sp")
    dp_count = lax.axis_size("dp")
    members = sp_count // 4
    cells = slab_rows * width
    size = cells // CHUNKS
    lanes = channels // 2
    x = frames_in.reshape(cells, channels)
    cot = cotangent.reshape(cells, channels)
    w3 = spatial_weight.reshape(3, 3 * channels, channels)
    scale = 1.0 / math.sqrt(slab_rows * sp_count * dp_count * width)

    count = 12 * channels
    block = 3 * channels
    blocks = 4 * SPLIT
    half, piece = block // SPLIT // 2, block // SPLIT // 8
    exchanges = blocks * (14 + members - 1)
    frame = jax.ShapeDtypeStruct((cells, channels), BF16)
    slab = pltpu.VMEM((cells, channels), BF16)
    padded = pltpu.VMEM((cells + 2 * width, 3 * channels), BF16)
    vmem = pl.BlockSpec(memory_space=pltpu.VMEM)
    hbm = pl.BlockSpec(memory_space=pltpu.HBM)
    block_out, grad_in, grads = pl.pallas_call(
        functools.partial(block_kernel, width, members, scale),
        out_shape=(slab, slab, pltpu.VMEM((count, channels), BF16)),
        in_specs=[hbm] * 4,
        out_specs=(vmem,) * 3,
        scratch_shapes=[slab] * 7
        + [
            pltpu.VMEM((cells, channels), F32),
            padded,
            padded,
            pltpu.VMEM((3, block, channels), BF16),
            pltpu.VMEM((3, channels, channels), BF16),
            pltpu.VMEM((3, block, channels), BF16),
            pltpu.VMEM((3, channels, channels), BF16),
            pltpu.VMEM((size, channels), F32),
            pltpu.VMEM((channels, size), BF16),
            pltpu.VMEM((3, block, size), BF16),
            pltpu.VMEM((count, channels), F32),
            pltpu.VMEM((count, lanes), F32),
            pltpu.VMEM((count, lanes), F32),
            pltpu.VMEM((count, lanes), BF16),
            pltpu.VMEM((blocks, half, lanes), BF16),
            pltpu.VMEM((blocks, 3, 2 * piece, lanes), BF16),
            pltpu.VMEM((blocks, members, piece, lanes), BF16),
            pltpu.SemaphoreType.DMA((4,)),
        ]
        + [pltpu.SemaphoreType.DMA((CHUNKS,))] * 10
        + [pltpu.SemaphoreType.DMA((exchanges,))] * 2,
        compiler_params=pltpu.CompilerParams(
            collective_id=0, has_side_effects=True, vmem_limit_bytes=VMEM_LIMIT
        ),
        cost_estimate=pl.CostEstimate(
            flops=72 * cells * channels * channels,
            bytes_accessed=16 * cells * channels,
            transcendentals=2 * cells * channels,
        ),
        name="video_block",
    )(x, cot, w3, temporal_weight)

    block_out, grad_in, grad_spatial, grad_temporal = pl.pallas_call(
        finish_kernel,
        out_shape=(
            frame, frame,
            jax.ShapeDtypeStruct((9 * channels, channels), F32),
            jax.ShapeDtypeStruct((3 * channels, channels), F32),
        ),
        in_specs=[vmem] * 3,
        out_specs=(hbm,) * 4,
        scratch_shapes=[pltpu.VMEM((count, channels), F32), pltpu.SemaphoreType.DMA((6,))],
        compiler_params=pltpu.CompilerParams(vmem_limit_bytes=16 * 1024 * 1024),
        name="finish",
    )(block_out, grad_in, grads)
    grad_spatial = grad_spatial.reshape(3, 3, channels, channels)
    grad_temporal = grad_temporal.reshape(3, channels, channels)
    return (
        block_out.reshape(frames_in.shape),
        grad_in.reshape(frames_in.shape),
        grad_spatial,
        grad_temporal,
    )


def solution(mesh):
    placed = (P(("dp", "sp"), None, None), P(), P(), P(("dp", "sp"), None, None))
    return jax.shard_map(
        local,
        mesh=mesh,
        in_specs=placed,
        out_specs=(P(("dp", "sp"), None, None), P(("dp", "sp"), None, None), P(), P()),
        check_vma=False,
    )
```

```python
import functools
import math

import jax
import jax.numpy as jnp
from jax import lax
from jax.experimental import pallas as pl
from jax.experimental.pallas import tpu as pltpu
from jax.sharding import PartitionSpec as P

FRAMES = 4
CHUNKS = 8
HALF = CHUNKS // 2
LEAD = CHUNKS // 8
VIA = 3
HOLD = 1
Z_FIRST = (0,)
SPLIT = 1
X_FIRST_AT = ((0.5, 0.6), (3.5, 2.1), (8.0, 2.1), (10.8, 2.1), (15.2, 2.1), (18.0, 2.1))
Z_FIRST_AT = ((0.5, 0.6), (8.0, 0.6), (11.0, 0.6), (13.8, 0.6), (18.3, 2.1), (20.9, 2.1))
HELD_AT = (17.3,)
GRAD_INPUT_AT = ((1, 3.0), (0, 3.1))
RELAY_AT = (2.5, 12.0, 21.6)
NOW = 2
LAST_AT = (5.0, 17.2, 19.6)
OWN_AT = 3.2
OLD_AT = ((9.0, 4, 6), (11.5, 6, 8), (13.6, 0, 2), (15.9, 2, 3), (19.7, 3, 4))
OUTPUT_AT = ((15.28, 4, 5), (17.38, 5, 6), (19.28, 6, 7), (21.28, 0, 1), (23.28, 7, 8), (28.1, 1, 2), (28.2, 3, 4), (28.3, 2, 3))
VMEM_LIMIT = 50 * 1024 * 1024
MESH = pl.DeviceIdType.MESH
F32 = jnp.float32
BF16 = jnp.bfloat16


def mm(left, right):
    return jnp.dot(left, right, preferred_element_type=F32)


def store_shifted(dest, offset, values, width):
    cells, channels = values.shape
    column = lax.broadcasted_iota(jnp.int32, (cells, channels), 0) % width
    before = jnp.where(column == 0, 0.0, pltpu.roll(values, 1, axis=0))
    after = jnp.where(column == width - 1, 0.0, pltpu.roll(values, cells - 1, axis=0))
    dest[pl.ds(offset, cells), 0:channels] = before.astype(BF16)
    dest[pl.ds(offset, cells), channels : 2 * channels] = values.astype(BF16)
    dest[pl.ds(offset, cells), 2 * channels : 3 * channels] = after.astype(BF16)


def zero_edges(dest, width):
    rows, lanes = dest.shape
    dest[0:width] = jnp.zeros((width, lanes), BF16)
    dest[rows - width : rows] = jnp.zeros((width, lanes), BF16)


def block_kernel(
    width, members, scale,
    x_hbm, cot_hbm, w_hbm, tw_hbm,
    out, gin, full,
    x, cot, c1, c2, a1, a2, act, slope, x3, g3, w_ref, tw_ref, wf, wt, part, act_last, x_last, acc,
    core_in, total, stage, x_in, z_in, slots,
    load_sem, c1_sem, c2_sem, a1_sem, a2_sem, cy_sem, cz_sem, ay_sem, az_sem, rc_sem, ra_sem,
    red_send, red_recv,
):
    dp = lax.axis_index("dp")
    sp = lax.axis_index("sp")
    frame = sp % FRAMES
    y = sp % 2
    zi = (sp // 2) % 4
    group = sp // 8
    member = y + 2 * group
    core = dp % 2
    mx = (dp // 2) % 2
    cells, channels = x.shape
    size = cells // CHUNKS
    lanes = channels // 2

    y_dev = (dp, sp + 1 - 2 * y)
    t_dev = (dp, sp + 2 - 4 * (zi % 2))
    core_dev = (dp + 1 - 2 * core, sp)
    x_dev = (dp + 2 - 4 * mx, sp)

    def z_member(offset):
        return (zi + offset) % 4

    def z_dev(offset):
        return (dp, sp + (z_member(offset) - zi) * 2)

    def m_dev(offset):
        other = (member + offset) % members
        return (dp, sp + other % 2 - y + (other // 2 - group) * 8)

    def chunk(ref, index):
        return ref.at[pl.ds(pl.multiple_of(index * size, size), size), :]

    def copy(source, dest, send_sem, recv_sem, device):
        return pltpu.make_async_remote_copy(
            src_ref=source, dst_ref=dest, send_sem=send_sem, recv_sem=recv_sem,
            device_id=device, device_id_type=MESH,
        )

    def send(source, dest, index, send_sems, recv_sems, device):
        copy(
            chunk(source, index), chunk(dest, index), send_sems.at[index], recv_sems.at[index], device
        ).start()

    def arrived(dest, index, recv_sems):
        copy(
            chunk(dest, index), chunk(dest, index), recv_sems.at[index], recv_sems.at[index], y_dev
        ).wait_recv()

    def left(index, send_sems):
        copy(
            chunk(act, index), chunk(act, index), send_sems.at[index], send_sems.at[index], y_dev
        ).wait_send()

    def each(start, stop, body):
        def step(index, carry):
            body(index)
            return carry

        lax.fori_loop(start, stop, step, 0)

    x_load = pltpu.make_async_copy(x_hbm, x, load_sem.at[0])
    cot_load = pltpu.make_async_copy(cot_hbm, cot, load_sem.at[1])
    w_load = pltpu.make_async_copy(w_hbm, w_ref, load_sem.at[2])
    tw_load = pltpu.make_async_copy(tw_hbm, tw_ref, load_sem.at[3])
    for load in (x_load, w_load, tw_load, cot_load):
        load.start()

    barrier = pltpu.get_barrier_semaphore()
    greeted = [core_dev, x_dev] + [z_dev(i) for i in (1, 2, 3)] + [m_dev(i) for i in range(1, members)]
    for device in greeted:
        pl.semaphore_signal(barrier, inc=1, device_id=device, device_id_type=MESH)
    pl.semaphore_wait(barrier, len(greeted))

    @pl.when(frame == 1)
    def _():
        each(0, CHUNKS, lambda i: send(cot_hbm, c1, i, cy_sem, c1_sem, y_dev))

    @pl.when(frame == 2)
    def _():
        each(0, CHUNKS, lambda i: send(cot_hbm, c2, i, cz_sem, c2_sem, t_dev))
        each(HALF, CHUNKS, lambda i: send(cot_hbm, c1, i, cy_sem, c1_sem, y_dev))

    @pl.when(frame == 3)
    def _():
        each(0, CHUNKS, lambda i: send(cot_hbm, c1, i, cy_sem, c1_sem, y_dev))
        each(0, HALF, lambda i: send(cot_hbm, c2, i, cz_sem, c2_sem, t_dev))

    acc[...] = jnp.zeros_like(acc)
    zero_edges(x3, width)
    zero_edges(g3, width)
    x_load.wait()
    w_load.wait()

    def forward(step):
        @pl.when(step < CHUNKS)
        def _():
            store_shifted(
                x3, pl.multiple_of(width + step * size, width),
                x[pl.ds(pl.multiple_of(step * size, size), size), :].astype(F32), width,
            )

        @pl.when(step >= 1)
        def _():
            index = step - 1
            base = pl.multiple_of(index * size, size)
            pre = jnp.zeros((size, channels), F32)
            for tap in range(3):
                pre = pre + mm(x3[pl.ds(base + tap * width, size), :], w_ref[tap])
            sigma = jax.nn.sigmoid(pre)
            act[pl.ds(base, size), :] = (pre * sigma).astype(BF16)
            slope[pl.ds(base, size), :] = sigma * (1.0 + pre * (1.0 - sigma))

            @pl.when(frame == 0)
            def _():
                send(act, a2, index, az_sem, a2_sem, t_dev)

            @pl.when((frame == 0) & (index < LEAD))
            def _():
                send(act, a1, index, ay_sem, a1_sem, y_dev)

            @pl.when((frame == 1) & (index < VIA))
            def _():
                send(act, a1, index, ay_sem, a1_sem, y_dev)

            @pl.when((frame == 1) & (index >= HALF))
            def _():
                send(act, a2, index, az_sem, a2_sem, t_dev)

            @pl.when((frame == 2) & (index < CHUNKS - HOLD))
            def _():
                send(act, a1, index, ay_sem, a1_sem, y_dev)

    each(0, CHUNKS + 1, forward)

    @pl.when(frame == 1)
    def _():
        each(0, HALF, lambda i: send(act, a2, HALF - 1 - i, az_sem, a2_sem, t_dev))

    tw_load.wait()
    for tap in range(3):
        wt[tap] = tw_ref[tap].T
        for side in range(3):
            wf[tap, side * channels : (side + 1) * channels, :] = w_ref[
                2 - tap, (2 - side) * channels : (3 - side) * channels, :
            ].T
    cot_load.wait()

    gt_base = 9 * channels
    block = 3 * channels

    def add_temporal(tap, act_t, other):
        acc[gt_base + tap * channels : gt_base + (tap + 1) * channels, :] += mm(act_t, other)

    def receive(index):
        rows = pl.ds(pl.multiple_of(index * size, size), size)
        early = index < HALF

        @pl.when((frame < 3) | (index >= HALF))
        def _():
            arrived(c1, index, c1_sem)

        @pl.when((frame == 0) | ((frame == 1) & early))
        def _():
            arrived(c2, index, c2_sem)

        @pl.when((frame == 0) & early)
        def _():
            send(c2, c1, index, rc_sem, c1_sem, y_dev)

        @pl.when((frame == 0) & (index == HALF - 1))
        def _():
            each(LEAD, CHUNKS - HOLD, lambda i: send(act, a1, i, ay_sem, a1_sem, y_dev))

        @pl.when((frame == 3) & (index >= HALF))
        def _():
            c2[rows, :] = (mm(c1[rows, :], wt[1]) + mm(cot[rows, :], wt[2])).astype(BF16)
            send(c2, c1, index, cz_sem, c1_sem, t_dev)

    def own_gradient(index):
        rows = pl.ds(pl.multiple_of(index * size, size), size)
        act_t = act[rows, :].T
        part[...] = mm(cot[rows, :], wt[0])
        add_temporal(0, act_t, cot[rows, :])
        return act_t

    def backward(index, finish, last=False):
        base = pl.multiple_of(index * size, size)
        rows = pl.ds(base, size)
        early = index < HALF
        act_t = act_last[...] if last else own_gradient(index)

        @pl.when((frame == 0) | (frame == 2) | ((frame == 1) & early))
        def _():
            part[...] += mm(c1[rows, :], wt[1])
            add_temporal(1, act_t, c1[rows, :])

        @pl.when((frame == 0) | ((frame == 1) & early))
        def _():
            part[...] += mm(c2[rows, :], wt[2])
            add_temporal(2, act_t, c2[rows, :])

        finish(0)

        @pl.when((frame == 1) & (index >= HALF))
        def _():
            part[...] += c1[rows, :].astype(F32)

        grad_pre = part[...].astype(BF16).astype(F32) * slope[rows, :]
        store_shifted(g3, pl.multiple_of(width + base, width), grad_pre, width)
        grad_pre = grad_pre.astype(BF16)
        for tap in range(3):
            window_t = x_last[tap] if last else x3[pl.ds(base + tap * width, size), :].T
            acc[tap * block : (tap + 1) * block, :] += mm(window_t, grad_pre)
            finish(1 + tap)

    def grad_input(index):
        base = pl.multiple_of(index * size, size)
        total_in = cot[pl.ds(base, size), :].astype(F32)
        for tap in range(3):
            total_in = total_in + mm(g3[pl.ds(base + tap * width, size), :], wf[tap])
        gin[pl.ds(base, size), :] = total_in.astype(BF16)

    def own_term(index):
        rows = pl.ds(pl.multiple_of(index * size, size), size)
        slope[rows, :] = mm(act[rows, :], tw_ref[0])

    def old_term(index):
        rows = pl.ds(pl.multiple_of(index * size, size), size)

        @pl.when((frame == 2) | ((frame == 3) & (index < VIA)))
        def _():
            arrived(a2, index, a2_sem)

        @pl.when(frame >= 2)
        def _():
            slope[rows, :] += mm(a2[rows, :], tw_ref[2])

    def output(index):
        rows = pl.ds(pl.multiple_of(index * size, size), size)

        def write(temporal):
            temporal = temporal.astype(BF16).astype(F32)
            out[rows, :] = (x[rows, :].astype(F32) + temporal).astype(BF16)

        @pl.when(frame == 0)
        def _():
            write(slope[rows, :])

        @pl.when(frame >= 1)
        def _():
            arrived(a1, index, a1_sem)
            write(slope[rows, :] + mm(a1[rows, :], tw_ref[1]))

    def relay_first(index):
        @pl.when(frame == 0)
        def _():
            arrived(a1, index, a1_sem)
            send(a1, a1, index, ra_sem, a1_sem, t_dev)

    def relay_last(index):
        @pl.when(frame == 3)
        def _():
            if index < HALF:
                arrived(a2, index, a2_sem)
            send(a2, a1, index, ra_sem, a1_sem, y_dev)

    def held(index):
        @pl.when((frame == 0) | (frame == 2))
        def _():
            send(act, a1, index, ay_sem, a1_sem, y_dev)

    span = block // SPLIT
    half, piece = span // 2, span // 8
    keep = pl.multiple_of(core * lanes, lanes)
    give = pl.multiple_of((1 - core) * lanes, lanes)
    mine = pl.ds(keep, lanes)
    bases = [
        start + part_of * span
        for start in [gt_base] + [tap * block for tap in range(3)]
        for part_of in range(SPLIT)
    ]
    used = []
    moving = {}

    def exchange(name, source, dest, device):
        slot = len(used)
        used.append(slot)
        moved = copy(source, dest, red_send.at[slot], red_recv.at[slot], device)
        moved.start()
        moving.setdefault(name, []).append(moved)

    def landed(name):
        for moved in moving.pop(name):
            moved.wait()

    def rows_of(start, length):
        return pl.ds(pl.multiple_of(start, 16), length)

    def half_of(which, part_x):
        return rows_of(bases[which] + part_x * half, half)

    def piece_of(which, offset):
        if which in Z_FIRST:
            return rows_of(bases[which] + z_member(offset) * 2 * piece + mx * piece, piece)
        return rows_of(bases[which] + mx * half + z_member(offset) * piece, piece)

    def pair_of(which, offset):
        return rows_of(bases[which] + z_member(offset) * 2 * piece, 2 * piece)

    def spread(name, rows, device):
        place = full.at[rows, mine]
        exchange(name, place, place, device)

    def to_core(which):
        rows = rows_of(bases[which], span)
        exchange(("core", which), acc.at[rows, pl.ds(give, lanes)], core_in.at[rows, :], core_dev)

    def to_first(which):
        landed(("core", which))
        rows = rows_of(bases[which], span)
        summed = acc[rows, mine] + core_in[rows, :]
        total[rows, :] = summed
        stage[rows, :] = summed.astype(BF16)
        if which in Z_FIRST:
            for offset in (2, 1, 3):
                exchange(
                    ("first", which), stage.at[pair_of(which, offset), :],
                    z_in.at[which, offset - 1], z_dev(offset),
                )
        else:
            exchange(
                ("first", which), stage.at[half_of(which, 1 - mx), :],
                x_in.at[which], x_dev,
            )

    def to_second(which):
        landed(("first", which))
        if which in Z_FIRST:
            rows = pair_of(which, 0)
            summed = total[rows, :]
            for offset in range(3):
                summed = summed + z_in[which, offset].astype(F32)
        else:
            rows = half_of(which, mx)
            summed = total[rows, :] + x_in[which].astype(F32)
        total[rows, :] = summed
        stage[rows, :] = summed.astype(BF16)
        if which in Z_FIRST:
            other = rows_of(bases[which] + zi * 2 * piece + (1 - mx) * piece, piece)
            exchange(
                ("second", which), stage.at[other, :], x_in.at[which, 0:piece, :], x_dev
            )
        else:
            for offset in (2, 1, 3):
                exchange(
                    ("second", which), stage.at[piece_of(which, offset), :],
                    z_in.at[which, offset - 1, 0:piece, :], z_dev(offset),
                )

    def to_y(which):
        landed(("second", which))
        summed = total[piece_of(which, 0), :]
        if which in Z_FIRST:
            summed = summed + x_in[which, 0:piece, :].astype(F32)
        else:
            for offset in range(3):
                summed = summed + z_in[which, offset, 0:piece, :].astype(F32)
        slots[which, member] = summed.astype(BF16)
        place = slots.at[which, member]
        for offset in range(1, members):
            exchange(("y", which), place, place, m_dev(offset))

    def back_z(which):
        landed(("y", which))
        summed = slots[which, 0].astype(F32)
        for other in range(1, members):
            summed = summed + slots[which, other].astype(F32)
        full[piece_of(which, 0), mine] = (summed * scale).astype(BF16)
        for offset in (2, 1, 3):
            spread(("backz", which), piece_of(which, 0), z_dev(offset))
        spread(("backx", which), piece_of(which, 0), x_dev)

    def back_x(which):
        landed(("backz", which))
        for offset in (2, 3, 1):
            spread(("backx", which), piece_of(which, offset), x_dev)
        if which not in Z_FIRST:
            spread(("last", which), half_of(which, mx), core_dev)

    def back_core(which):
        landed(("backx", which))
        if which in Z_FIRST:
            spread(("last", which), rows_of(bases[which], span), core_dev)
        else:
            spread(("last", which), half_of(which, 1 - mx), core_dev)

    def fill_in(index):
        receive(index)
        backward(index, lambda which: None)

        @pl.when(index >= 1)
        def _():
            grad_input(index - 1)

        own_term(index)

    each(0, CHUNKS - 1, fill_in)
    act_last[...] = own_gradient(CHUNKS - 1)
    for tap in range(3):
        start = (CHUNKS - 1) * size + tap * width
        x_last[tap] = x3[start : start + size, :].T
    receive(CHUNKS - 1)

    @pl.when(frame == 3)
    def _():
        def late(index):
            rows = pl.ds(pl.multiple_of(index * size, size), size)
            arrived(a2, index, a2_sem)

            @pl.when(index < HALF + NOW)
            def _():
                send(a2, a1, index, ra_sem, a1_sem, y_dev)

            act_t = a2[rows, :].T
            add_temporal(1, act_t, c1[rows, :])
            add_temporal(2, act_t, cot[rows, :])

        each(HALF, CHUNKS, late)

    def all_to_core(which):
        for part_of in range(SPLIT):
            to_core(which * SPLIT + part_of)

    backward(CHUNKS - 1, all_to_core, last=True)

    later = []
    actions = (to_first, to_second, to_y, back_z, back_x, back_core)
    for which in range(4 * SPLIT):
        times = Z_FIRST_AT if which in Z_FIRST else X_FIRST_AT
        for action, (when, stride) in zip(actions, times):
            later.append((when + stride * which / SPLIT, action, which))
    for index, when in GRAD_INPUT_AT:
        later.append((when, grad_input, CHUNKS - 1 - index))
    later.append((OWN_AT, own_term, CHUNKS - 1))
    for when, start, stop in OLD_AT:
        later.append((when, lambda span: each(span[0], span[1], old_term), (start, stop)))
    for index, when in enumerate(RELAY_AT):
        later.append((when, relay_first, index))
    waiting = [*range(HALF + NOW, CHUNKS), *range(HALF - 1, VIA - 1, -1)]
    for index, when in zip(waiting, LAST_AT):
        later.append((when, relay_last, index))
    for index, when in enumerate(HELD_AT):
        later.append((when, held, CHUNKS - HOLD + index))
    for when, start, stop in OUTPUT_AT:
        later.append((when, lambda span: each(span[0], span[1], output), (start, stop)))
    for _, action, argument in sorted(later, key=lambda entry: entry[0]):
        action(argument)
    for which in range(4 * SPLIT):
        landed(("last", which))

    @pl.when(frame == 0)
    def _():
        each(0, HALF, lambda i: left(i, rc_sem))
        each(0, VIA, lambda i: left(i, ra_sem))
        each(0, CHUNKS, lambda i: left(i, ay_sem))
        each(0, CHUNKS, lambda i: left(i, az_sem))

    @pl.when(frame == 1)
    def _():
        each(0, CHUNKS, lambda i: left(i, cy_sem))
        each(0, VIA, lambda i: left(i, ay_sem))
        each(0, CHUNKS, lambda i: left(i, az_sem))

    @pl.when(frame == 2)
    def _():
        each(0, CHUNKS, lambda i: left(i, cz_sem))
        each(HALF, CHUNKS, lambda i: left(i, cy_sem))
        each(0, CHUNKS, lambda i: left(i, ay_sem))

    @pl.when(frame == 3)
    def _():
        each(0, CHUNKS, lambda i: left(i, cy_sem))
        each(0, CHUNKS, lambda i: left(i, cz_sem))
        each(VIA, CHUNKS, lambda i: left(i, ra_sem))


def finish_kernel(
    out, gin, grads, out_hbm, gin_hbm, spatial_hbm, temporal_hbm, wide, sems
):
    block = grads.shape[0] // 4
    stores = []

    def store(source, dest):
        stores.append(pltpu.make_async_copy(source, dest, sems.at[len(stores)]))
        stores[-1].start()

    store(out, out_hbm)
    store(gin, gin_hbm)
    for index in range(4):
        part = pl.ds(index * block, block)
        wide[part, :] = grads[part, :].astype(F32)
        store(wide.at[part, :], spatial_hbm.at[part, :] if index < 3 else temporal_hbm)
    for move in stores:
        move.wait()


def local(frames_in, spatial_weight, temporal_weight, cotangent):
    slab_rows, width, channels = frames_in.shape
    sp_count = lax.axis_size("sp")
    dp_count = lax.axis_size("dp")
    members = sp_count // 4
    cells = slab_rows * width
    size = cells // CHUNKS
    lanes = channels // 2
    x = frames_in.reshape(cells, channels)
    cot = cotangent.reshape(cells, channels)
    w3 = spatial_weight.reshape(3, 3 * channels, channels)
    scale = 1.0 / math.sqrt(slab_rows * sp_count * dp_count * width)

    count = 12 * channels
    block = 3 * channels
    blocks = 4 * SPLIT
    half, piece = block // SPLIT // 2, block // SPLIT // 8
    exchanges = blocks * (14 + members - 1)
    frame = jax.ShapeDtypeStruct((cells, channels), BF16)
    slab = pltpu.VMEM((cells, channels), BF16)
    padded = pltpu.VMEM((cells + 2 * width, 3 * channels), BF16)
    vmem = pl.BlockSpec(memory_space=pltpu.VMEM)
    hbm = pl.BlockSpec(memory_space=pltpu.HBM)
    block_out, grad_in, grads = pl.pallas_call(
        functools.partial(block_kernel, width, members, scale),
        out_shape=(slab, slab, pltpu.VMEM((count, channels), BF16)),
        in_specs=[hbm] * 4,
        out_specs=(vmem,) * 3,
        scratch_shapes=[slab] * 7
        + [
            pltpu.VMEM((cells, channels), F32),
            padded,
            padded,
            pltpu.VMEM((3, block, channels), BF16),
            pltpu.VMEM((3, channels, channels), BF16),
            pltpu.VMEM((3, block, channels), BF16),
            pltpu.VMEM((3, channels, channels), BF16),
            pltpu.VMEM((size, channels), F32),
            pltpu.VMEM((channels, size), BF16),
            pltpu.VMEM((3, block, size), BF16),
            pltpu.VMEM((count, channels), F32),
            pltpu.VMEM((count, lanes), F32),
            pltpu.VMEM((count, lanes), F32),
            pltpu.VMEM((count, lanes), BF16),
            pltpu.VMEM((blocks, half, lanes), BF16),
            pltpu.VMEM((blocks, 3, 2 * piece, lanes), BF16),
            pltpu.VMEM((blocks, members, piece, lanes), BF16),
            pltpu.SemaphoreType.DMA((4,)),
        ]
        + [pltpu.SemaphoreType.DMA((CHUNKS,))] * 10
        + [pltpu.SemaphoreType.DMA((exchanges,))] * 2,
        compiler_params=pltpu.CompilerParams(
            collective_id=0, has_side_effects=True, vmem_limit_bytes=VMEM_LIMIT
        ),
        cost_estimate=pl.CostEstimate(
            flops=72 * cells * channels * channels,
            bytes_accessed=16 * cells * channels,
            transcendentals=2 * cells * channels,
        ),
        name="video_block",
    )(x, cot, w3, temporal_weight)

    block_out, grad_in, grad_spatial, grad_temporal = pl.pallas_call(
        finish_kernel,
        out_shape=(
            frame, frame,
            jax.ShapeDtypeStruct((9 * channels, channels), F32),
            jax.ShapeDtypeStruct((3 * channels, channels), F32),
        ),
        in_specs=[vmem] * 3,
        out_specs=(hbm,) * 4,
        scratch_shapes=[pltpu.VMEM((count, channels), F32), pltpu.SemaphoreType.DMA((6,))],
        compiler_params=pltpu.CompilerParams(vmem_limit_bytes=16 * 1024 * 1024),
        name="finish",
    )(block_out, grad_in, grads)
    grad_spatial = grad_spatial.reshape(3, 3, channels, channels)
    grad_temporal = grad_temporal.reshape(3, channels, channels)
    return (
        block_out.reshape(frames_in.shape),
        grad_in.reshape(frames_in.shape),
        grad_spatial,
        grad_temporal,
    )


def solution(mesh):
    placed = (P(("dp", "sp"), None, None), P(), P(), P(("dp", "sp"), None, None))
    return jax.shard_map(
        local,
        mesh=mesh,
        in_specs=placed,
        out_specs=(P(("dp", "sp"), None, None), P(("dp", "sp"), None, None), P(), P()),
        check_vma=False,
    )
```
